128 devices in a mesh: replica: 4 (over z), fsdp: 32 (over x, y, core).
Axes of the slice: x: 4, y: 4, z: 4, core: 2. Of those that a mesh axis runs over, the one named last changes fastest.
Arguments:
- weight: float32 [4096, 128, 128], P('fsdp'), may hold values from -6 to 6
- moment: float32 [4096, 128, 128], P('fsdp'), may hold values from -6 to 6
- base_codes: int32 [4096, 128, 128], P('fsdp'), may hold values from -8 to 7
- base_scale: float32 [4096], P('fsdp'), may hold values from 0.05 to 0.2
- weight_mask: int32 [4096], P('fsdp'), may hold values 0 or 1
- moment_mask: int32 [4096], P('fsdp'), may hold values 0 or 1
- writer: int32 [4096, 1], P('fsdp'), may hold values from 0 to 31; in each aligned block of 128 rows (0 to 127, 128 to 255, ...) at most 8 rows name the same one
Outputs:
- written_weight: bfloat16 [1024, 8, 128, 128], P('fsdp')
- written_moment: bfloat16 [1024, 8, 128, 128], P('fsdp')
- written_scales: bfloat16 [2, 1024, 8], P(None, 'fsdp')
- refreshed: bfloat16 [4096, 128, 128], P('fsdp')
The draws below stay inside these ranges and needn't reach their ends.
Inputs may be any that keep to these rules, and one draw needn't show every extreme that they name: No writer is named by more than 8 blocks of one fsdp shard.
All inputs are finite; a program needn't handle non-finite values. Where the reference program divides by a largest or mean magnitude, that divisor is 1e-20 or more. No bound on the sum of `weight_mask` or of `moment_mask` on one device may be relied on, other than what follows from the above.
Results may differ from the reference program's by a relative error of at most 0.013.
Values may be sent and summed in bfloat16 or wider, within the bound.
No kernel may reach another device: no remote copies, remote signals or barrier semaphores. Data moves between devices by JAX's collectives and lax.ppermute only.
A program may use at most 192 MiB of HBM per device.

```python
import math
import jax
import jax.numpy as jnp
import numpy as np

BS = 128
BLK_DEV = 128
CAP = 8
NB = 4096
N_FSDP = 32


def with_ends(array, stream_key, smallest, top_value):
    spot = [jax.random.randint(jax.random.fold_in(stream_key, axis), (), 0, length) for axis, length in enumerate(array.shape)]
    widest = array.shape.index(max(array.shape))
    neighbour = spot[:widest] + [(spot[widest] + 1) % array.shape[widest]] + spot[widest + 1:]
    return array.at[tuple(spot)].set(smallest).at[tuple(neighbour)].set(top_value)


def block_levels(rng, dims, pieces, smallest, largest):
    level, own = 1.0, jax.random.fold_in(rng, 6)
    for dim, parts in pieces:
        draws = jnp.exp(jax.random.uniform(jax.random.fold_in(own, dim), (parts,), jnp.float32, smallest / len(pieces), largest / len(pieces)))
        level = level * jnp.repeat(draws, dims[dim] // parts).reshape([-1 if axis == dim else 1 for axis in range(len(dims))])
    return level


def assign_block(stream_key, own, number, rows, number_of, top, most, lean):
    order = jax.random.permutation(stream_key, number_of)
    packed, usual = load_shares(number_of, rows * top, most, lean, True), load_shares(number_of, rows * top, most, lean, False)
    places = jnp.arange(number_of)

    def named(lengths, offset_by):
        used = int((lengths > 0).sum())
        fixed = max(1, used // 4)
        passed = fixed + (places - fixed + offset_by * (used - fixed)) % max(1, number_of - fixed)
        return jnp.zeros((number_of,), jnp.int32).at[order[jnp.where(places < fixed, places, passed)]].set(jnp.asarray(lengths, jnp.int32))

    lengths = jnp.where(number % 4 == 0, named(packed, number // 4), named(usual, number - number // 4 - 1))
    mixed = jax.random.permutation(jax.random.fold_in(own, 3), number_of)
    source_of, sink = mixed[0:number_of // 2 * 2:2], mixed[1:number_of // 2 * 2:2]
    slack = jnp.minimum(lengths[source_of] - 1, most - lengths[sink]) // 2
    slack = jnp.where((source_of == order[0]) | (sink == order[0]) | (lengths[sink] == 0), 0, jnp.maximum(slack, 0))
    passed = jax.random.randint(jax.random.fold_in(own, 4), (number_of // 2,), 0, 1 << 20) % (slack + 1)
    lengths = lengths.at[source_of].add(-passed).at[sink].add(passed)
    members = jnp.searchsorted(jnp.cumsum(lengths), jnp.arange(rows * top), side="right").astype(jnp.int32)
    listing = members.reshape(top, rows).T
    listing = listing[jax.random.permutation(jax.random.fold_in(own, 1), rows)]
    offset_by = jax.random.randint(jax.random.fold_in(own, 2), (rows, 1), 0, top)
    return jnp.take_along_axis(listing, (jnp.arange(top)[None, :] + offset_by) % top, axis=1)


def load_shares(amount, total, reach, skew, full):
    weights = [(1 << 20) // math.isqrt(grade ** skew) + 1 for grade in range(1, amount + 1)]
    largest = reach if full else min(reach, max(-(-total // amount), total * weights[0] // sum(weights)))
    least = 1 if total - largest >= amount - 1 else 0
    holding, spare = [largest] + [least] * (amount - 1), total - largest - least * (amount - 1)
    while spare > 0:
        movable = [i for i in range(1, amount) if holding[i] < largest] or [i for i in range(1, amount) if holding[i] < reach]
        pool, left = sum([weights[i] for i in movable]), spare
        for i in movable:
            addition = min(reach - holding[i], max(1, left * weights[i] // pool), spare)
            holding[i] = holding[i] + addition
            spare = spare - addition
    return np.array(holding)


def bell_draw(key, extent, deviation, bound, cuts=(), kind=jnp.bfloat16):
    loudness = block_levels(key, extent, cuts, -0.22, 0.18) if cuts else 1.0
    values = jax.random.normal(key, extent, jnp.float32) * deviation * loudness
    return jnp.minimum(jnp.maximum(values, -bound), bound).astype(kind)


def setup_inputs(seed: int = 0) -> dict:
    splits = jax.random.split(jax.random.key(seed), 8)
    weight = bell_draw(splits[0], (NB, BS, BS), 1.0, 6.0, ((0, 32),), jnp.float32)
    moment = bell_draw(splits[1], (NB, BS, BS), 1.0, 6.0, ((0, 32),), jnp.float32)
    base_codes = with_ends(jax.random.randint(splits[2], (NB, BS, BS), -8, 8), jax.random.fold_in(splits[2], 1), -8, 7).astype(jnp.int32)
    base_scale = jnp.clip(jnp.exp(math.log(0.2) - 1.3862944 * jax.random.uniform(splits[3], (NB,), jnp.float32) ** block_levels(splits[3], (NB,), ((0, 32),), -0.2, 0.2)), 0.05, 0.2)
    weight_mask = with_ends((jax.random.randint(splits[4], (NB,), 0, 2) < 1).astype(jnp.int32), jax.random.fold_in(splits[4], 1), 0, 1)
    moment_mask = with_ends((jax.random.randint(splits[5], (NB,), 0, 3) < 2).astype(jnp.int32), jax.random.fold_in(splits[5], 1), 0, 1)
    writer_keys = jax.random.split(jax.random.fold_in(splits[6], 1), NB // BLK_DEV)
    writer_turns = jax.random.permutation(jax.random.fold_in(splits[6], 3), NB // BLK_DEV)
    writer = jax.vmap(lambda own, number: assign_block(jax.random.fold_in(splits[6], 2), own, number, BLK_DEV, N_FSDP, 1, CAP, 2))(writer_keys, writer_turns).reshape((NB, 1))
    return {"weight": weight, "moment": moment, "base_codes": base_codes, "base_scale": base_scale, "weight_mask": weight_mask, "moment_mask": moment_mask, "writer": writer}


EPSILON = 1e-6


def compress(weights_in, moment_in, codes_in, scale_in, wmask_in, mmask_in):
    base_value = codes_in.astype(jnp.float32) * scale_in[:, None, None]
    residual = weights_in - base_value
    keep_weight = wmask_in.astype(jnp.float32)
    keep_moment = (wmask_in * mmask_in).astype(jnp.float32)
    scale_weight = (jnp.max(jnp.abs(residual), axis=(1, 2)) + EPSILON).astype(jnp.bfloat16)
    scale_moment = (jnp.max(jnp.abs(moment_in), axis=(1, 2)) + EPSILON).astype(jnp.bfloat16)
    coded_weight = (residual / scale_weight.astype(jnp.float32)[:, None, None] * keep_weight[:, None, None]).astype(jnp.bfloat16)
    coded_moment = (moment_in / scale_moment.astype(jnp.float32)[:, None, None] * keep_moment[:, None, None]).astype(jnp.bfloat16)
    refreshed = (base_value + coded_weight.astype(jnp.float32) * scale_weight.astype(jnp.float32)[:, None, None]).astype(jnp.bfloat16)
    return coded_weight, coded_moment, scale_weight, scale_moment, refreshed


def reference(weight, moment, base_codes, base_scale, weight_mask, moment_mask, writer):
    coded_weight, coded_moment, scale_weight, scale_moment, refreshed = compress(weight, moment, base_codes, base_scale, weight_mask, moment_mask)
    target = writer[:, 0].astype(jnp.int32)
    source = (jnp.arange(NB, dtype=jnp.int32) // BLK_DEV).astype(jnp.int32)
    onehot = (target[:, None] == jnp.arange(N_FSDP, dtype=jnp.int32)[None, :]).astype(jnp.int32)
    onehot = onehot.reshape(N_FSDP, BLK_DEV, N_FSDP)
    before = jnp.cumsum(onehot, axis=1).astype(jnp.int32) - onehot
    slot_rank = jnp.sum(before * onehot, axis=2).reshape(NB).astype(jnp.int32)
    destination = ((target * N_FSDP + source) * CAP + slot_rank).astype(jnp.int32)
    total = N_FSDP * N_FSDP * CAP
    written_weight = jnp.zeros((total, BS, BS), jnp.bfloat16).at[destination].set(coded_weight)
    written_moment = jnp.zeros((total, BS, BS), jnp.bfloat16).at[destination].set(coded_moment)
    written_scales = jnp.zeros((2, total), jnp.bfloat16)
    written_scales = written_scales.at[0, destination].set(scale_weight).at[1, destination].set(scale_moment)
    return (written_weight.reshape(N_FSDP * N_FSDP, CAP, BS, BS),
            written_moment.reshape(N_FSDP * N_FSDP, CAP, BS, BS),
            written_scales.reshape(2, N_FSDP * N_FSDP, CAP),
            refreshed)
```

```python
import functools

import jax
import jax.numpy as jnp
from jax import lax
from jax.experimental import pallas as pl
from jax.experimental.pallas import tpu as pltpu
from jax.sharding import PartitionSpec as P

EPSILON = 1e-06
WRITERS = 32
CAP = 8
GROUP = 8
ROWS = 32
VMEM = 60 * 1024 * 1024

SLOTS_MOMENT = (3, 3, 2)
SLOTS_WEIGHT = (3, 2, 3)


def start_map(step, blocks, slot_of, count, coded):
    @pl.when(step == 0)
    def _():
        def clear(i, carry):
            slot_of[i] = blocks
            return carry

        def clear_count(i, carry):
            count[i] = 0
            return carry

        lax.fori_loop(0, WRITERS * CAP, clear, 0, unroll=8)
        lax.fori_loop(0, WRITERS, clear_count, 0, unroll=8)
        coded[blocks] = jnp.zeros(coded.shape[1:], coded.dtype)


def note_block(block, writer, slot_of, count):
    target = writer[block]
    rank = count[target]
    count[target] = rank + 1
    slot_of[target * CAP + rank] = block


def scale_of(values):
    top = jnp.max(jnp.max(jnp.abs(values), axis=0, keepdims=True), axis=1, keepdims=True)
    top = jnp.broadcast_to(top + EPSILON, (8, 128))
    return top.astype(jnp.bfloat16).astype(jnp.float32)


def place(step, steps, replica, slots, slot_of, coded, first, second, whole):
    @pl.when(step == steps - 1)
    def _():
        rows = pl.ds(pl.multiple_of(replica[0] * ROWS, ROWS), ROWS)
        n_first, n_second, n_whole = slots

        def one(w, carry):
            for k in range(n_first):
                first[w * n_first + k] = coded[slot_of[w * CAP + k], rows, :]
            for k in range(n_second):
                second[w * n_second + k] = coded[slot_of[w * CAP + n_first + k], rows, :]
            for k in range(n_whole):
                whole[w * n_whole + k] = coded[slot_of[w * CAP + n_first + n_second + k]]
            return carry

        lax.fori_loop(0, WRITERS, one, 0, unroll=2)


def moment_kernel(blocks, slots, replica, writer, weight_mask, moment_mask, moment, first, second, whole, scales, coded, slot_of, count):
    step = pl.program_id(0)
    start_map(step, blocks, slot_of, count, coded)
    for i in range(GROUP):
        block = step * GROUP + i
        note_block(block, writer, slot_of, count)
        keep = (weight_mask[block] * moment_mask[block]).astype(jnp.float32)
        values = moment[i]
        scale = scale_of(values)
        scales[pl.ds(i, 1), :] = scale[0:1, :]
        coded[block] = (values * (keep / scale)[0:1, :]).astype(jnp.bfloat16)
    place(step, blocks // GROUP, replica, slots, slot_of, coded, first, second, whole)


def weight_kernel(
    blocks, slots, replica, writer, weight_mask, base_scale, weight, codes, first, second, whole, scales, refreshed, coded, slot_of, count
):
    step = pl.program_id(0)
    start_map(step, blocks, slot_of, count, coded)
    for i in range(GROUP):
        block = step * GROUP + i
        note_block(block, writer, slot_of, count)
        keep = weight_mask[block].astype(jnp.float32)
        base = codes[i].astype(jnp.float32) * base_scale[block]
        values = weight[i] - base
        scale = scale_of(values)
        scales[pl.ds(i, 1), :] = scale[0:1, :]
        rounded = (values * (keep / scale)[0:1, :]).astype(jnp.bfloat16)
        coded[block] = rounded
        refreshed[i] = (base + rounded.astype(jnp.float32) * scale[0:1, :]).astype(jnp.bfloat16)
    place(step, blocks // GROUP, replica, slots, slot_of, coded, first, second, whole)


def compress_call(kernel, slots, scalars, arrays, refresh, cost):
    blocks, width = arrays[0].shape[0], arrays[0].shape[1]
    steps = blocks // GROUP
    bf16 = jnp.bfloat16
    shapes = [
        jax.ShapeDtypeStruct((WRITERS * slots[0], ROWS, width), bf16),
        jax.ShapeDtypeStruct((WRITERS * slots[1], ROWS, width), bf16),
        jax.ShapeDtypeStruct((WRITERS * slots[2], width, width), bf16),
        jax.ShapeDtypeStruct((blocks, 128), jnp.float32),
    ]
    specs = [pl.BlockSpec(s.shape, lambda i, *_: (0, 0, 0)) for s in shapes[:3]]
    specs.append(pl.BlockSpec((GROUP, 128), lambda i, *_: (i, 0)))
    moving = pl.BlockSpec((GROUP, width, width), lambda i, *_: (i, 0, 0))
    if refresh:
        shapes.append(jax.ShapeDtypeStruct((blocks, width, width), bf16))
        specs.append(moving)
    return pl.pallas_call(
        functools.partial(kernel, blocks, slots),
        grid_spec=pltpu.PrefetchScalarGridSpec(
            num_scalar_prefetch=len(scalars),
            grid=(steps,),
            in_specs=[moving] * len(arrays),
            out_specs=specs,
            scratch_shapes=[
                pltpu.VMEM((blocks + 1, width, width), bf16),
                pltpu.SMEM((WRITERS * CAP,), jnp.int32),
                pltpu.SMEM((WRITERS,), jnp.int32),
            ],
        ),
        out_shape=shapes,
        compiler_params=pltpu.CompilerParams(dimension_semantics=("arbitrary",), vmem_limit_bytes=VMEM),
        cost_estimate=pl.CostEstimate(flops=cost[0], bytes_accessed=cost[1], transcendentals=0),
    )(*scalars, *arrays)


SOURCES = 4


def unpack_kernel(slots, replica, *refs):
    quarters, whole, out = (refs[0:4], refs[4:8]), refs[8], refs[9]
    for turn in range(4):
        rows = pl.ds(pl.multiple_of(lax.rem(replica[0] + turn, 4) * ROWS, ROWS), ROWS)
        for s in range(SOURCES):
            for k in range(slots[0]):
                out[s * CAP + k, rows, :] = quarters[0][turn][s * slots[0] + k]
            for k in range(slots[1]):
                out[s * CAP + slots[0] + k, rows, :] = quarters[1][turn][s * slots[1] + k]
    for s in range(SOURCES):
        for k in range(slots[2]):
            out[s * CAP + slots[0] + slots[1] + k] = whole[s * slots[2] + k]


def unpack_call(slots, replica, first, second, whole):
    width = whole.shape[-1]

    def spec(n, rows):
        return pl.BlockSpec((SOURCES * n, rows, width), lambda i, *_: (i, 0, 0))

    return pl.pallas_call(
        functools.partial(unpack_kernel, slots),
        grid_spec=pltpu.PrefetchScalarGridSpec(
            num_scalar_prefetch=1,
            grid=(WRITERS // SOURCES,),
            in_specs=[spec(slots[0], ROWS)] * 4 + [spec(slots[1], ROWS)] * 4 + [spec(slots[2], width)],
            out_specs=spec(CAP, width),
        ),
        out_shape=jax.ShapeDtypeStruct((WRITERS * CAP, width, width), jnp.bfloat16),
        compiler_params=pltpu.CompilerParams(dimension_semantics=("arbitrary",), vmem_limit_bytes=VMEM),
        cost_estimate=pl.CostEstimate(flops=0, bytes_accessed=1 << 24, transcendentals=0),
    )(replica, *first, *second, whole)


def regroup(values):
    return lax.all_to_all(values, "fsdp", split_axis=0, concat_axis=0, tiled=True)


def upward(values):
    return lax.ppermute(values, "replica", [(i, (i + 1) % 4) for i in range(4)])


def downward(values):
    return lax.ppermute(values, "replica", [(i, (i - 1) % 4) for i in range(4)])


def gather_rows(first, second):
    first_up, first_down = upward(first), downward(first)
    second_up, second_down = upward(second), downward(second)
    return (
        (first, first_down, upward(first_up), first_up),
        (second, second_down, downward(second_down), second_up),
    )


def on_device(weight, moment, base_codes, base_scale, weight_mask, moment_mask, writer):
    blocks, width = weight.shape[0], weight.shape[1]
    target = writer[:, 0]
    replica = lax.axis_index("replica").astype(jnp.int32).reshape(1)
    m_first, m_second, m_whole, m_scales = compress_call(
        moment_kernel, SLOTS_MOMENT, (replica, target, weight_mask, moment_mask), (moment,), False, (10 << 20, 12 << 20)
    )
    w_first, w_second, w_whole, w_scales, refreshed = compress_call(
        weight_kernel, SLOTS_WEIGHT, (replica, target, weight_mask, base_scale), (weight, base_codes), True, (20 << 20, 24 << 20)
    )
    m_first, m_second = regroup(m_first), regroup(m_second)
    w_first, w_second = regroup(w_first), regroup(w_second)
    m_whole, w_whole = regroup(m_whole), regroup(w_whole)
    m_parts = gather_rows(m_first, m_second)
    w_parts = gather_rows(w_first, w_second)

    onehot = (target[:, None] == jnp.arange(WRITERS, dtype=jnp.int32)[None, :]).astype(jnp.int32)
    rank = jnp.sum((jnp.cumsum(onehot, axis=0) - onehot) * onehot, axis=1)
    slot = target * CAP + rank
    matches = slot[:, None] == jnp.arange(WRITERS * CAP, dtype=jnp.int32)[None, :]
    by_slot = [jnp.sum(jnp.where(matches, s[:, 0:1], 0.0), axis=0).reshape(WRITERS, CAP) for s in (w_scales, m_scales)]
    got_scales = regroup(jnp.concatenate(by_slot, axis=1).astype(jnp.bfloat16))
    written_scales = jnp.transpose(got_scales.reshape(WRITERS, 2, CAP), (1, 0, 2))

    written_moment = unpack_call(SLOTS_MOMENT, replica, *m_parts, m_whole)
    written_weight = unpack_call(SLOTS_WEIGHT, replica, *w_parts, w_whole)
    shape = (WRITERS, CAP, width, width)
    return written_weight.reshape(shape), written_moment.reshape(shape), written_scales, refreshed


def solution(mesh):
    placed = (
        P("fsdp", None, None),
        P("fsdp", None, None),
        P("fsdp", None, None),
        P("fsdp"),
        P("fsdp"),
        P("fsdp"),
        P("fsdp", None),
    )
    return jax.shard_map(
        on_device,
        mesh=mesh,
        in_specs=placed,
        out_specs=(
            P("fsdp", None, None, None),
            P("fsdp", None, None, None),
            P(None, "fsdp", None),
            P("fsdp", None, None),
        ),
        check_vma=False,
    )
```

```python
import functools

import jax
import jax.numpy as jnp
from jax import lax
from jax.experimental import pallas as pl
from jax.experimental.pallas import tpu as pltpu
from jax.sharding import PartitionSpec as P

EPSILON = 1e-06
WRITERS = 32
CAP = 8
GROUP = 8
ROWS = 32
TILE = 16
SLOTS = WRITERS * CAP
VMEM = 60 * 1024 * 1024

BY_ROWS_MOMENT = 8
BY_ROWS_WEIGHT = 6
USUAL = (128, 128)
FULL = (WRITERS * BY_ROWS_MOMENT + 8, WRITERS * BY_ROWS_WEIGHT + 8)


def clear(ref, length, value):
    def one(i, carry):
        ref[i] = value
        return carry

    lax.fori_loop(0, length, one, 0, unroll=8)


def scale_of(values):
    top = jnp.max(jnp.max(jnp.abs(values), axis=0, keepdims=True), axis=1, keepdims=True)
    top = jnp.broadcast_to(top + EPSILON, (8, 128))
    return top.astype(jnp.bfloat16).astype(jnp.float32)


def row_quarter(replica):
    return pl.ds(pl.multiple_of(replica[0] * ROWS, ROWS), ROWS)


def payload_rows(by_rows):
    return by_rows * ROWS + TILE


def tile_rows(writer, by_rows):
    return pl.ds(pl.multiple_of(writer * payload_rows(by_rows) + by_rows * ROWS, TILE), TILE)


def slot_rows(writer, k, by_rows):
    return pl.ds(pl.multiple_of(writer * payload_rows(by_rows) + k * ROWS, TILE), ROWS)


def moment_kernel(blocks, replica, writer, weight_mask, moment_mask, moment, payload, coded, scales, slot_of, kept_w, kept_m, count, count_w, count_m):
    step = pl.program_id(0)
    rows = row_quarter(replica)

    @pl.when(step == 0)
    def _():
        clear(slot_of, SLOTS, blocks)
        clear(kept_w, SLOTS, 0)
        clear(kept_m, SLOTS, 0)
        clear(count, WRITERS, 0)
        clear(count_w, WRITERS, 0)
        clear(count_m, WRITERS, 0)
        coded[blocks] = jnp.zeros(coded.shape[1:], coded.dtype)
        scales[pl.ds(blocks, 8), :] = jnp.zeros((8, 128), jnp.float32)

    for i in range(GROUP):
        block = step * GROUP + i
        target = writer[block]
        rank = count[target]
        count[target] = rank + 1
        slot = target * CAP + rank
        slot_of[slot] = block
        keep_w = weight_mask[block]
        keep_m = keep_w * moment_mask[block]
        kept_w[slot] = keep_w
        kept_m[slot] = keep_m
        count_w[target] = count_w[target] + jnp.where(rank < BY_ROWS_WEIGHT, keep_w, 0)
        count_m[target] = count_m[target] + jnp.where(rank < BY_ROWS_MOMENT, keep_m, 0)
        scale = scale_of(moment[i])
        scales[pl.ds(block, 1), :] = scale[0:1, :]
        coded[block] = (moment[i, rows, :] * (keep_m.astype(jnp.float32) / scale)[0:1, :]).astype(jnp.bfloat16)

    @pl.when(step == blocks // GROUP - 1)
    def _():
        lane = lax.broadcasted_iota(jnp.int32, (TILE, 128), 1)
        line = lax.broadcasted_iota(jnp.int32, (TILE, 128), 0)

        def counts(w, tile):
            both = jnp.where(line == 3, count_w[w].astype(jnp.float32), jnp.where(line == 4, count_m[w].astype(jnp.float32), 0.0))
            return jnp.where(lane == w, both, tile)

        common = lax.fori_loop(0, WRITERS, counts, jnp.zeros((TILE, 128), jnp.float32))

        def one(w, carry):
            tile = common
            for k in range(CAP):
                slot = w * CAP + k
                block = slot_of[slot]
                if k < BY_ROWS_MOMENT:
                    payload[slot_rows(w, k, BY_ROWS_MOMENT), :] = coded[block]
                scale = jnp.broadcast_to(scales[pl.ds(block, 1), :], (TILE, 128))
                kept = jnp.where(line == 1, kept_w[slot].astype(jnp.float32), kept_m[slot].astype(jnp.float32))
                tile = jnp.where((lane == k) & (line <= 2), jnp.where(line == 0, scale, kept), tile)
            payload[tile_rows(w, BY_ROWS_MOMENT), :] = tile.astype(jnp.bfloat16)
            return carry

        lax.fori_loop(0, WRITERS, one, 0)


def weight_kernel(blocks, replica, writer, weight_mask, base_scale, weight, codes, payload, whole, refreshed, coded, scales, slot_of, count):
    step = pl.program_id(0)

    @pl.when(step == 0)
    def _():
        clear(slot_of, SLOTS, blocks)
        clear(count, WRITERS, 0)
        coded[blocks] = jnp.zeros(coded.shape[1:], coded.dtype)
        scales[pl.ds(blocks, 8), :] = jnp.zeros((8, 128), jnp.float32)

    for i in range(GROUP):
        block = step * GROUP + i
        target = writer[block]
        rank = count[target]
        count[target] = rank + 1
        slot_of[target * CAP + rank] = block
        keep = weight_mask[block].astype(jnp.float32)
        base = codes[i].astype(jnp.float32) * base_scale[block]
        values = weight[i] - base
        scale = scale_of(values)
        scales[pl.ds(block, 1), :] = scale[0:1, :]
        rounded = (values * (keep / scale)[0:1, :]).astype(jnp.bfloat16)
        coded[block] = rounded
        refreshed[i] = (base + rounded.astype(jnp.float32) * scale[0:1, :]).astype(jnp.bfloat16)

    @pl.when(step == blocks // GROUP - 1)
    def _():
        rows = row_quarter(replica)
        lane = lax.broadcasted_iota(jnp.int32, (TILE, 128), 1)

        def one(w, carry):
            tile = jnp.zeros((TILE, 128), jnp.float32)
            for k in range(CAP):
                block = slot_of[w * CAP + k]
                if k < BY_ROWS_WEIGHT:
                    payload[slot_rows(w, k, BY_ROWS_WEIGHT), :] = coded[block, rows, :]
                else:
                    whole[w * (CAP - BY_ROWS_WEIGHT) + k - BY_ROWS_WEIGHT] = coded[block]
                tile = jnp.where(lane == k, jnp.broadcast_to(scales[pl.ds(block, 1), :], (TILE, 128)), tile)
            payload[tile_rows(w, BY_ROWS_WEIGHT), :] = tile.astype(jnp.bfloat16)
            return carry

        lax.fori_loop(0, WRITERS, one, 0)


def cost(flops, moved):
    return pl.CostEstimate(flops=flops, bytes_accessed=moved, transcendentals=0)


def params():
    return pltpu.CompilerParams(dimension_semantics=("arbitrary",), vmem_limit_bytes=VMEM)


def moment_call(replica, writer, weight_mask, moment_mask, moment):
    blocks, width = moment.shape[0], moment.shape[1]
    shape = (WRITERS * payload_rows(BY_ROWS_MOMENT), width)
    return pl.pallas_call(
        functools.partial(moment_kernel, blocks),
        grid_spec=pltpu.PrefetchScalarGridSpec(
            num_scalar_prefetch=4,
            grid=(blocks // GROUP,),
            in_specs=[pl.BlockSpec((GROUP, width, width), lambda i, *_: (i, 0, 0))],
            out_specs=pl.BlockSpec(shape, lambda i, *_: (0, 0)),
            scratch_shapes=[
                pltpu.VMEM((blocks + 1, ROWS, width), jnp.bfloat16),
                pltpu.VMEM((blocks + 8, 128), jnp.float32),
                pltpu.SMEM((SLOTS,), jnp.int32),
                pltpu.SMEM((SLOTS,), jnp.int32),
                pltpu.SMEM((SLOTS,), jnp.int32),
                pltpu.SMEM((WRITERS,), jnp.int32),
                pltpu.SMEM((WRITERS,), jnp.int32),
                pltpu.SMEM((WRITERS,), jnp.int32),
            ],
        ),
        out_shape=jax.ShapeDtypeStruct(shape, jnp.bfloat16),
        compiler_params=params(),
        cost_estimate=cost(10 << 20, 12 << 20),
    )(replica, writer, weight_mask, moment_mask, moment)


def weight_call(replica, writer, weight_mask, base_scale, weight, codes):
    blocks, width = weight.shape[0], weight.shape[1]
    moving = pl.BlockSpec((GROUP, width, width), lambda i, *_: (i, 0, 0))
    payload = (WRITERS * payload_rows(BY_ROWS_WEIGHT), width)
    whole = (WRITERS * (CAP - BY_ROWS_WEIGHT), width, width)
    return pl.pallas_call(
        functools.partial(weight_kernel, blocks),
        grid_spec=pltpu.PrefetchScalarGridSpec(
            num_scalar_prefetch=4,
            grid=(blocks // GROUP,),
            in_specs=[moving, moving],
            out_specs=[pl.BlockSpec(payload, lambda i, *_: (0, 0)), pl.BlockSpec(whole, lambda i, *_: (0, 0, 0)), moving],
            scratch_shapes=[
                pltpu.VMEM((blocks + 1, width, width), jnp.bfloat16),
                pltpu.VMEM((blocks + 8, 128), jnp.float32),
                pltpu.SMEM((SLOTS,), jnp.int32),
                pltpu.SMEM((WRITERS,), jnp.int32),
            ],
        ),
        out_shape=[
            jax.ShapeDtypeStruct(payload, jnp.bfloat16),
            jax.ShapeDtypeStruct(whole, jnp.bfloat16),
            jax.ShapeDtypeStruct((blocks, width, width), jnp.bfloat16),
        ],
        compiler_params=params(),
        cost_estimate=cost(20 << 20, 28 << 20),
    )(replica, writer, weight_mask, base_scale, weight, codes)


def pack_kernel(by_rows, half, kept, payload, _, first, second, passed, packed):
    def one(s, place):
        for k in range(by_rows):
            packed[place] = payload[slot_rows(s, k, by_rows), :]
            place = place + kept[s * CAP + k]
        return place

    lax.fori_loop(0, WRITERS, one, 0)
    first[...] = packed[0:half]
    second[...] = packed[half : 2 * half]


def pack_call(by_rows, capacity, kept, payload, later):
    width = payload.shape[-1]
    half = capacity // 2
    part = (half, ROWS, width)
    return pl.pallas_call(
        functools.partial(pack_kernel, by_rows, half),
        grid_spec=pltpu.PrefetchScalarGridSpec(
            num_scalar_prefetch=1,
            grid=(1,),
            in_specs=[pl.BlockSpec(payload.shape, lambda i, *_: (0, 0)), pl.BlockSpec(memory_space=pl.ANY)],
            out_specs=[pl.BlockSpec(part, lambda i, *_: (0, 0, 0))] * 2 + [pl.BlockSpec(memory_space=pl.ANY)],
            scratch_shapes=[pltpu.VMEM((capacity, ROWS, width), jnp.bfloat16)],
        ),
        out_shape=[jax.ShapeDtypeStruct(part, jnp.bfloat16)] * 2 + [jax.ShapeDtypeStruct(later.shape, later.dtype)],
        input_output_aliases={2: 2},
        compiler_params=params(),
        cost_estimate=cost(0, 4 << 20),
    )(kept, payload, later)


SOURCES = 4


def unpack_kernel(by_rows, half, replica, kept, *refs):
    parts, refs = refs[:8], refs[8:]
    if by_rows < CAP:
        whole, refs = refs[0], refs[1:]
    out, held, sems, place_ref = refs
    step = pl.program_id(0)

    @pl.when(step == 0)
    def _():
        place_ref[0] = 0
        copies = [
            pltpu.make_async_copy(part, held.at[i // 2, pl.ds((i % 2) * half, half)], sems.at[i]) for i, part in enumerate(parts)
        ]
        for copy in copies:
            copy.start()
        for copy in copies:
            copy.wait()

    rows = [pl.ds(pl.multiple_of(lax.rem(replica[0] + turn, 4) * ROWS, ROWS), ROWS) for turn in range(4)]
    place = place_ref[0]
    for s in range(SOURCES):
        for k in range(by_rows):
            flag = kept[(step * SOURCES + s) * CAP + k]
            for turn in range(4):
                values = held[turn, place]
                out[s * CAP + k, rows[turn], :] = jnp.where(flag > 0, values, jnp.zeros_like(values))
            place = place + flag
        for k in range(by_rows, CAP):
            out[s * CAP + k] = whole[s * (CAP - by_rows) + k - by_rows]
    place_ref[0] = place


def unpack_call(by_rows, capacity, replica, kept, parts, whole):
    width = parts[0].shape[-1]
    half = capacity // 2
    specs = [pl.BlockSpec(memory_space=pl.ANY)] * 8
    if whole is not None:
        specs.append(pl.BlockSpec((SOURCES * (CAP - by_rows), width, width), lambda i, *_: (i, 0, 0)))
        parts = (*parts, whole)
    return pl.pallas_call(
        functools.partial(unpack_kernel, by_rows, half),
        grid_spec=pltpu.PrefetchScalarGridSpec(
            num_scalar_prefetch=2,
            grid=(WRITERS // SOURCES,),
            in_specs=specs,
            out_specs=pl.BlockSpec((SOURCES * CAP, width, width), lambda i, *_: (i, 0, 0)),
            scratch_shapes=[
                pltpu.VMEM((4, capacity, ROWS, width), jnp.bfloat16),
                pltpu.SemaphoreType.DMA((8,)),
                pltpu.SMEM((1,), jnp.int32),
            ],
        ),
        out_shape=jax.ShapeDtypeStruct((SLOTS, width, width), jnp.bfloat16),
        compiler_params=params(),
        cost_estimate=cost(0, 14 << 20),
    )(replica, kept, *parts)


def regroup(values):
    return lax.all_to_all(values, "fsdp", split_axis=0, concat_axis=0, tiled=True)


def upward(values):
    return lax.ppermute(values, "replica", [(i, (i + 1) % 4) for i in range(4)])


def downward(values):
    return lax.ppermute(values, "replica", [(i, (i - 1) % 4) for i in range(4)])


def gather_rows(first, second):
    first_up, first_down = upward(first), downward(first)
    second_up, second_down = upward(second), downward(second)
    return (first, second, first_down, second_down, upward(first_up), downward(second_down), first_up, second_up)


def exchange(capacities, replica, kept_w, kept_m, m_payload, w_payload, w_whole):
    m_first, m_second, w_payload = pack_call(BY_ROWS_MOMENT, capacities[0], kept_m, m_payload, w_payload)
    m_parts = gather_rows(m_first, m_second)
    w_payload = regroup(w_payload)
    w_first, w_second, w_whole = pack_call(BY_ROWS_WEIGHT, capacities[1], kept_w, w_payload, w_whole)
    w_parts = gather_rows(w_first, w_second)
    w_whole = regroup(w_whole)
    written_moment = unpack_call(BY_ROWS_MOMENT, capacities[0], replica, kept_m, m_parts, None)
    written_weight = unpack_call(BY_ROWS_WEIGHT, capacities[1], replica, kept_w, w_parts, w_whole)
    w_tile = w_payload.reshape(WRITERS, payload_rows(BY_ROWS_WEIGHT), -1)[:, BY_ROWS_WEIGHT * ROWS, :CAP]
    return written_weight, written_moment, w_tile


def on_device(weight, moment, base_codes, base_scale, weight_mask, moment_mask, writer):
    width = weight.shape[1]
    target = writer[:, 0]
    replica = lax.axis_index("replica").astype(jnp.int32).reshape(1)
    m_payload = regroup(moment_call(replica, target, weight_mask, moment_mask, moment))
    w_payload, w_whole, refreshed = weight_call(replica, target, weight_mask, base_scale, weight, base_codes)

    tile = m_payload.reshape(WRITERS, payload_rows(BY_ROWS_MOMENT), width)[:, BY_ROWS_MOMENT * ROWS :, :]
    kept_w, kept_m = (tile[:, line, :CAP].astype(jnp.int32).reshape(SLOTS) for line in (1, 2))
    totals = jnp.sum(tile[:, 3:5, :WRITERS].astype(jnp.int32), axis=0)
    fits = jnp.all(totals < jnp.array([[USUAL[1]], [USUAL[0]]], jnp.int32))
    written_weight, written_moment, w_scales = lax.cond(
        fits,
        functools.partial(exchange, USUAL),
        functools.partial(exchange, FULL),
        replica, kept_w, kept_m, m_payload, w_payload, w_whole,
    )
    written_scales = jnp.stack([w_scales, tile[:, 0, :CAP]], axis=0)
    shape = (WRITERS, CAP, width, width)
    return written_weight.reshape(shape), written_moment.reshape(shape), written_scales, refreshed


def solution(mesh):
    placed = (
        P("fsdp", None, None),
        P("fsdp", None, None),
        P("fsdp", None, None),
        P("fsdp"),
        P("fsdp"),
        P("fsdp"),
        P("fsdp", None),
    )
    return jax.shard_map(
        on_device,
        mesh=mesh,
        in_specs=placed,
        out_specs=(
            P("fsdp", None, None, None),
            P("fsdp", None, None, None),
            P(None, "fsdp", None),
            P("fsdp", None, None),
        ),
        check_vma=False,
    )
```

```python
import functools

import jax
import jax.numpy as jnp
from jax import lax
from jax.experimental import pallas as pl
from jax.experimental.pallas import tpu as pltpu
from jax.sharding import PartitionSpec as P

EPSILON = 1e-06
WRITERS = 32
CAP = 8
GROUP = 8
GROUP_MOMENT = 16
ROWS = 32
TILE = 16
SLOTS = WRITERS * CAP
VMEM = 60 * 1024 * 1024

BY_ROWS_MOMENT = 8
BY_ROWS_WEIGHT = 6
USUAL = (128, 128)
FULL = (WRITERS * BY_ROWS_MOMENT + 8, WRITERS * BY_ROWS_WEIGHT + 8)


def clear(ref, length, value):
    def one(i, carry):
        ref[i] = value
        return carry

    lax.fori_loop(0, length, one, 0, unroll=8)


def scale_of(values):
    top = jnp.max(jnp.max(jnp.abs(values), axis=0, keepdims=True), axis=1, keepdims=True)
    top = jnp.broadcast_to(top + EPSILON, (8, 128))
    return top.astype(jnp.bfloat16).astype(jnp.float32)


def row_quarter(replica):
    return pl.ds(pl.multiple_of(replica[0] * ROWS, ROWS), ROWS)


def payload_rows(by_rows):
    return by_rows * ROWS + TILE


def tile_rows(writer, by_rows):
    return pl.ds(pl.multiple_of(writer * payload_rows(by_rows) + by_rows * ROWS, TILE), TILE)


def slot_rows(writer, k, by_rows):
    return pl.ds(pl.multiple_of(writer * payload_rows(by_rows) + k * ROWS, TILE), ROWS)


def moment_kernel(replica, writer, weight_mask, moment_mask, moment, payload, held, sems, tiles, totals, count):
    rows = row_quarter(replica)
    lane = lax.broadcasted_iota(jnp.int32, (8, 128), 1)
    line = lax.broadcasted_iota(jnp.int32, (8, 128), 0)
    steps = held.shape[0] // GROUP_MOMENT

    def fetch(step):
        part = pl.ds(step * GROUP_MOMENT, GROUP_MOMENT)
        return pltpu.make_async_copy(moment.at[part], held.at[part], sems.at[step])

    for step in range(steps):
        fetch(step).start()
    clear(count, WRITERS, 0)
    tiles[...] = jnp.zeros(tiles.shape, tiles.dtype)
    totals[...] = jnp.zeros(totals.shape, totals.dtype)

    def one_step(step, carry):
        fetch(step).wait()
        total = totals[...]
        for i in range(GROUP_MOMENT):
            block = step * GROUP_MOMENT + i
            target = writer[block]
            rank = count[target]
            count[target] = rank + 1
            keep_w = weight_mask[block].astype(jnp.float32)
            keep_m = keep_w * moment_mask[block].astype(jnp.float32)
            counted_w = jnp.where(rank < BY_ROWS_WEIGHT, keep_w, 0.0)
            total = total + jnp.where(lane == target, jnp.where(line == 3, counted_w, jnp.where(line == 4, keep_m, 0.0)), 0.0)
            scale = scale_of(held[block])
            kept = jnp.where(line == 0, scale, jnp.where(line == 1, keep_w, jnp.where(line == 2, keep_m, 0.0)))
            tiles[target] = jnp.where(lane == rank, kept, tiles[target])
            payload[slot_rows(target, rank, BY_ROWS_MOMENT), :] = (held[block, rows, :] * (keep_m / scale)[0:1, :]).astype(jnp.bfloat16)
        totals[...] = total
        return carry

    lax.fori_loop(0, steps, one_step, 0)
    common = totals[...]
    blank = jnp.zeros((TILE - 8, 128), jnp.float32)

    def one(w, carry):
        tile = jnp.concatenate([tiles[w] + common, blank], axis=0)
        payload[tile_rows(w, BY_ROWS_MOMENT), :] = tile.astype(jnp.bfloat16)
        return carry

    lax.fori_loop(0, WRITERS, one, 0, unroll=4)


def weight_kernel(blocks, replica, writer, weight_mask, base_scale, weight, codes, payload, whole, refreshed, coded, scales, slot_of, count):
    step = pl.program_id(0)

    @pl.when(step == 0)
    def _():
        clear(slot_of, SLOTS, blocks)
        clear(count, WRITERS, 0)
        coded[blocks] = jnp.zeros(coded.shape[1:], coded.dtype)
        scales[pl.ds(blocks, 8), :] = jnp.zeros((8, 128), jnp.float32)

    for i in range(GROUP):
        block = step * GROUP + i
        target = writer[block]
        rank = count[target]
        count[target] = rank + 1
        slot_of[target * CAP + rank] = block
        keep = weight_mask[block].astype(jnp.float32)
        base = codes[i].astype(jnp.float32) * base_scale[block]
        values = weight[i] - base
        scale = scale_of(values)
        scales[pl.ds(block, 1), :] = scale[0:1, :]
        rounded = (values * (keep / scale)[0:1, :]).astype(jnp.bfloat16)
        coded[block] = rounded
        refreshed[i] = (base + rounded.astype(jnp.float32) * scale[0:1, :]).astype(jnp.bfloat16)

    @pl.when(step == blocks // GROUP - 1)
    def _():
        rows = row_quarter(replica)
        lane = lax.broadcasted_iota(jnp.int32, (TILE, 128), 1)

        def one(w, carry):
            tile = jnp.zeros((TILE, 128), jnp.float32)
            for k in range(CAP):
                block = slot_of[w * CAP + k]
                if k < BY_ROWS_WEIGHT:
                    payload[slot_rows(w, k, BY_ROWS_WEIGHT), :] = coded[block, rows, :]
                else:
                    whole[w * (CAP - BY_ROWS_WEIGHT) + k - BY_ROWS_WEIGHT] = coded[block]
                tile = jnp.where(lane == k, jnp.broadcast_to(scales[pl.ds(block, 1), :], (TILE, 128)), tile)
            payload[tile_rows(w, BY_ROWS_WEIGHT), :] = tile.astype(jnp.bfloat16)
            return carry

        lax.fori_loop(0, WRITERS, one, 0)


def cost(flops, moved):
    return pl.CostEstimate(flops=flops, bytes_accessed=moved, transcendentals=0)


def params():
    return pltpu.CompilerParams(dimension_semantics=("arbitrary",), vmem_limit_bytes=VMEM)


def moment_call(replica, writer, weight_mask, moment_mask, moment):
    blocks, width = moment.shape[0], moment.shape[1]
    shape = (WRITERS * payload_rows(BY_ROWS_MOMENT), width)
    return pl.pallas_call(
        moment_kernel,
        grid_spec=pltpu.PrefetchScalarGridSpec(
            num_scalar_prefetch=4,
            grid=(1,),
            in_specs=[pl.BlockSpec(memory_space=pl.ANY)],
            out_specs=pl.BlockSpec(shape, lambda i, *_: (0, 0)),
            scratch_shapes=[
                pltpu.VMEM(moment.shape, jnp.float32),
                pltpu.SemaphoreType.DMA((blocks // GROUP_MOMENT,)),
                pltpu.VMEM((WRITERS, 8, 128), jnp.float32),
                pltpu.VMEM((8, 128), jnp.float32),
                pltpu.SMEM((WRITERS,), jnp.int32),
            ],
        ),
        out_shape=jax.ShapeDtypeStruct(shape, jnp.bfloat16),
        compiler_params=params(),
        cost_estimate=cost(10 << 20, 12 << 20),
    )(replica, writer, weight_mask, moment_mask, moment)


def weight_call(replica, writer, weight_mask, base_scale, weight, codes):
    blocks, width = weight.shape[0], weight.shape[1]
    moving = pl.BlockSpec((GROUP, width, width), lambda i, *_: (i, 0, 0))
    payload = (WRITERS * payload_rows(BY_ROWS_WEIGHT), width)
    whole = (WRITERS * (CAP - BY_ROWS_WEIGHT), width, width)
    return pl.pallas_call(
        functools.partial(weight_kernel, blocks),
        grid_spec=pltpu.PrefetchScalarGridSpec(
            num_scalar_prefetch=4,
            grid=(blocks // GROUP,),
            in_specs=[moving, moving],
            out_specs=[pl.BlockSpec(payload, lambda i, *_: (0, 0)), pl.BlockSpec(whole, lambda i, *_: (0, 0, 0)), moving],
            scratch_shapes=[
                pltpu.VMEM((blocks + 1, width, width), jnp.bfloat16),
                pltpu.VMEM((blocks + 8, 128), jnp.float32),
                pltpu.SMEM((SLOTS,), jnp.int32),
                pltpu.SMEM((WRITERS,), jnp.int32),
            ],
        ),
        out_shape=[
            jax.ShapeDtypeStruct(payload, jnp.bfloat16),
            jax.ShapeDtypeStruct(whole, jnp.bfloat16),
            jax.ShapeDtypeStruct((blocks, width, width), jnp.bfloat16),
        ],
        compiler_params=params(),
        cost_estimate=cost(20 << 20, 28 << 20),
    )(replica, writer, weight_mask, base_scale, weight, codes)


def pack_kernel(by_rows, half, kept, payload, *refs):
    first, second, _, packed = refs[-4:]

    def one(s, place):
        for k in range(by_rows):
            packed[place] = payload[slot_rows(s, k, by_rows), :]
            place = place + kept[s * CAP + k]
        return place

    lax.fori_loop(0, WRITERS, one, 0)
    first[...] = packed[0:half]
    second[...] = packed[half : 2 * half]


def pack_call(by_rows, capacity, kept, payload, later, earlier=()):
    width = payload.shape[-1]
    half = capacity // 2
    part = (half, ROWS, width)
    return pl.pallas_call(
        functools.partial(pack_kernel, by_rows, half),
        grid_spec=pltpu.PrefetchScalarGridSpec(
            num_scalar_prefetch=1,
            grid=(1,),
            in_specs=[pl.BlockSpec(payload.shape, lambda i, *_: (0, 0))] + [pl.BlockSpec(memory_space=pl.ANY)] * (1 + len(earlier)),
            out_specs=[pl.BlockSpec(part, lambda i, *_: (0, 0, 0))] * 2 + [pl.BlockSpec(memory_space=pl.ANY)],
            scratch_shapes=[pltpu.VMEM((capacity, ROWS, width), jnp.bfloat16)],
        ),
        out_shape=[jax.ShapeDtypeStruct(part, jnp.bfloat16)] * 2 + [jax.ShapeDtypeStruct(later.shape, later.dtype)],
        input_output_aliases={2: 2},
        compiler_params=params(),
        cost_estimate=cost(0, 4 << 20),
    )(kept, payload, later, *earlier)


SOURCES = 4


def unpack_kernel(by_rows, half, replica, kept, *refs):
    parts, refs = refs[:8], refs[8:]
    n_whole = CAP - by_rows
    if n_whole:
        whole, refs = refs[0], refs[1:]
    out, held, built, sems, out_sems = refs[:5]
    copies = [pltpu.make_async_copy(part, held.at[i // 2, pl.ds((i % 2) * half, half)], sems.at[i]) for i, part in enumerate(parts)]
    if n_whole:
        copies.append(pltpu.make_async_copy(whole, refs[5], sems.at[8]))
    for copy in copies:
        copy.start()
    for turn in range(4):
        held[turn, 2 * half] = jnp.zeros(held.shape[2:], held.dtype)
    for copy in copies:
        copy.wait()
    rows = [pl.ds(pl.multiple_of(lax.rem(replica[0] + turn, 4) * ROWS, ROWS), ROWS) for turn in range(4)]

    def send(step):
        part = pl.ds(step * SOURCES * CAP, SOURCES * CAP)
        return pltpu.make_async_copy(built.at[part], out.at[part], out_sems.at[step])

    def one(step, place):
        for s in range(SOURCES):
            source = step * SOURCES + s
            for k in range(by_rows):
                slot = source * CAP + k
                flag = kept[slot]
                origin = jnp.where(flag > 0, place, 2 * half)
                for turn in range(4):
                    built[slot, rows[turn], :] = held[turn, origin]
                place = place + flag
            for k in range(n_whole):
                built[source * CAP + by_rows + k] = refs[5][source * n_whole + k]
        send(step).start()
        return place

    steps = WRITERS // SOURCES
    lax.fori_loop(0, steps, one, 0)
    for step in range(steps):
        send(step).wait()


def unpack_call(by_rows, capacity, replica, kept, parts, whole):
    width = parts[0].shape[-1]
    half = capacity // 2
    scratch = [
        pltpu.VMEM((4, capacity + 1, ROWS, width), jnp.bfloat16),
        pltpu.VMEM((SLOTS, width, width), jnp.bfloat16),
        pltpu.SemaphoreType.DMA((9,)),
        pltpu.SemaphoreType.DMA((WRITERS // SOURCES,)),
    ]
    if whole is not None:
        parts = (*parts, whole)
        scratch.append(pltpu.VMEM(whole.shape, whole.dtype))
    return pl.pallas_call(
        functools.partial(unpack_kernel, by_rows, half),
        grid_spec=pltpu.PrefetchScalarGridSpec(
            num_scalar_prefetch=2,
            grid=(1,),
            in_specs=[pl.BlockSpec(memory_space=pl.ANY)] * len(parts),
            out_specs=pl.BlockSpec(memory_space=pl.ANY),
            scratch_shapes=scratch,
        ),
        out_shape=jax.ShapeDtypeStruct((SLOTS, width, width), jnp.bfloat16),
        compiler_params=params(),
        cost_estimate=cost(0, 14 << 20),
    )(replica, kept, *parts)


def regroup(values):
    return lax.all_to_all(values, "fsdp", split_axis=0, concat_axis=0, tiled=True)


def upward(values):
    return lax.ppermute(values, "replica", [(i, (i + 1) % 4) for i in range(4)])


def downward(values):
    return lax.ppermute(values, "replica", [(i, (i - 1) % 4) for i in range(4)])


def gather_rows(first, second):
    first_up, first_down = upward(first), downward(first)
    second_up, second_down = upward(second), downward(second)
    return (first, second, first_down, second_down, upward(first_up), downward(second_down), first_up, second_up)


def exchange(capacities, replica, kept_w, kept_m, m_payload, w_payload, w_whole):
    m_first, m_second, w_payload = pack_call(BY_ROWS_MOMENT, capacities[0], kept_m, m_payload, w_payload)
    m_parts = gather_rows(m_first, m_second)
    w_payload = regroup(w_payload)
    w_first, w_second, w_whole = pack_call(BY_ROWS_WEIGHT, capacities[1], kept_w, w_payload, w_whole, m_parts[2:])
    w_parts = gather_rows(w_first, w_second)
    w_whole = regroup(w_whole)
    written_moment = unpack_call(BY_ROWS_MOMENT, capacities[0], replica, kept_m, m_parts, None)
    written_weight = unpack_call(BY_ROWS_WEIGHT, capacities[1], replica, kept_w, w_parts, w_whole)
    w_tile = w_payload.reshape(WRITERS, payload_rows(BY_ROWS_WEIGHT), -1)[:, BY_ROWS_WEIGHT * ROWS, :CAP]
    return written_weight, written_moment, w_tile


def on_device(weight, moment, base_codes, base_scale, weight_mask, moment_mask, writer):
    width = weight.shape[1]
    target = writer[:, 0]
    replica = lax.axis_index("replica").astype(jnp.int32).reshape(1)
    m_payload = regroup(moment_call(replica, target, weight_mask, moment_mask, moment))
    w_payload, w_whole, refreshed = weight_call(replica, target, weight_mask, base_scale, weight, base_codes)

    tile = m_payload.reshape(WRITERS, payload_rows(BY_ROWS_MOMENT), width)[:, BY_ROWS_MOMENT * ROWS :, :]
    kept_w, kept_m = (tile[:, line, :CAP].astype(jnp.int32).reshape(SLOTS) for line in (1, 2))
    totals = jnp.sum(tile[:, 3:5, :WRITERS].astype(jnp.int32), axis=0)
    fits = jnp.all(totals < jnp.array([[USUAL[1]], [USUAL[0]]], jnp.int32))
    written_weight, written_moment, w_scales = lax.cond(
        fits,
        functools.partial(exchange, USUAL),
        functools.partial(exchange, FULL),
        replica, kept_w, kept_m, m_payload, w_payload, w_whole,
    )
    written_scales = jnp.stack([w_scales, tile[:, 0, :CAP]], axis=0)
    shape = (WRITERS, CAP, width, width)
    return written_weight.reshape(shape), written_moment.reshape(shape), written_scales, refreshed


def solution(mesh):
    placed = (
        P("fsdp", None, None),
        P("fsdp", None, None),
        P("fsdp", None, None),
        P("fsdp"),
        P("fsdp"),
        P("fsdp"),
        P("fsdp", None),
    )
    return jax.shard_map(
        on_device,
        mesh=mesh,
        in_specs=placed,
        out_specs=(
            P("fsdp", None, None, None),
            P("fsdp", None, None, None),
            P(None, "fsdp", None),
            P("fsdp", None, None),
        ),
        check_vma=False,
    )
```

```python
import functools

import jax
import jax.numpy as jnp
from jax import lax
from jax.experimental import pallas as pl
from jax.experimental.pallas import tpu as pltpu
from jax.sharding import PartitionSpec as P

EPSILON = 1e-06
WRITERS = 32
CAP = 8
GROUP = 8
GROUP_MOMENT = 16
ROWS = 32
TILE = 16
SLOTS = WRITERS * CAP
VMEM = 60 * 1024 * 1024

WHOLE = 2
BY_ROWS_MOMENT = CAP
BY_ROWS_WEIGHT = CAP - WHOLE
USUAL = (116, 96)
FULL = (WRITERS * BY_ROWS_MOMENT + 8, WRITERS * BY_ROWS_WEIGHT + 8)


def clear(ref, length, value):
    def one(i, carry):
        ref[i] = value
        return carry

    lax.fori_loop(0, length, one, 0, unroll=8)


def scale_of(values):
    top = jnp.max(jnp.max(jnp.abs(values), axis=0, keepdims=True), axis=1, keepdims=True)
    top = jnp.broadcast_to(top + EPSILON, (8, 128))
    return top.astype(jnp.bfloat16).astype(jnp.float32)


def row_quarter(replica):
    return pl.ds(pl.multiple_of(replica[0] * ROWS, ROWS), ROWS)


def payload_rows(by_rows):
    return by_rows * ROWS + TILE


def tile_rows(writer, by_rows):
    return pl.ds(pl.multiple_of(writer * payload_rows(by_rows) + by_rows * ROWS, TILE), TILE)


def slot_rows(writer, k, by_rows):
    return pl.ds(pl.multiple_of(writer * payload_rows(by_rows) + k * ROWS, TILE), ROWS)


def moment_kernel(replica, writer, weight_mask, moment_mask, moment, payload, held, sems, tiles, totals, count):
    rows = row_quarter(replica)
    lane = lax.broadcasted_iota(jnp.int32, (8, 128), 1)
    line = lax.broadcasted_iota(jnp.int32, (8, 128), 0)
    steps = held.shape[0] // GROUP_MOMENT

    def fetch(step):
        part = pl.ds(step * GROUP_MOMENT, GROUP_MOMENT)
        return pltpu.make_async_copy(moment.at[part], held.at[part], sems.at[step])

    for step in range(steps):
        fetch(step).start()
    clear(count, WRITERS, 0)
    tiles[...] = jnp.zeros(tiles.shape, tiles.dtype)
    totals[...] = jnp.zeros(totals.shape, totals.dtype)

    def one_step(step, carry):
        fetch(step).wait()
        total = totals[...]
        for i in range(GROUP_MOMENT):
            block = step * GROUP_MOMENT + i
            target = writer[block]
            rank = count[target]
            count[target] = rank + 1
            keep_w = weight_mask[block].astype(jnp.float32)
            keep_m = keep_w * moment_mask[block].astype(jnp.float32)
            total = total + jnp.where(lane == target, jnp.where(line == 3, keep_w, jnp.where(line == 4, keep_m, 0.0)), 0.0)
            scale = scale_of(held[block])
            kept = jnp.where(line == 0, scale, jnp.where(line == 1, keep_w, jnp.where(line == 2, keep_m, 0.0)))
            tiles[target] = jnp.where(lane == rank, kept, tiles[target])
            payload[slot_rows(target, rank, BY_ROWS_MOMENT), :] = (held[block, rows, :] * (keep_m / scale)[0:1, :]).astype(jnp.bfloat16)
        totals[...] = total
        return carry

    lax.fori_loop(0, steps, one_step, 0)
    common = totals[...]
    common = jnp.where(line == 3, jnp.maximum(common - WHOLE, 0.0), common)
    blank = jnp.zeros((TILE - 8, 128), jnp.float32)

    def one(w, carry):
        tile = jnp.concatenate([tiles[w] + common, blank], axis=0)
        payload[tile_rows(w, BY_ROWS_MOMENT), :] = tile.astype(jnp.bfloat16)
        return carry

    lax.fori_loop(0, WRITERS, one, 0, unroll=4)


def weight_kernel(blocks, replica, writer, weight_mask, base_scale, weight, codes, payload, whole, refreshed, coded, scales, slot_of, kept_of, count, count_kept):
    step = pl.program_id(0)

    @pl.when(step == 0)
    def _():
        clear(slot_of, SLOTS, blocks)
        clear(kept_of, SLOTS, blocks)
        clear(count, WRITERS, 0)
        clear(count_kept, WRITERS, 0)
        coded[blocks] = jnp.zeros(coded.shape[1:], coded.dtype)
        scales[pl.ds(blocks, 8), :] = jnp.zeros((8, 128), jnp.float32)

    for i in range(GROUP):
        block = step * GROUP + i
        target = writer[block]
        rank = count[target]
        count[target] = rank + 1
        slot_of[target * CAP + rank] = block
        rank_kept = count_kept[target]
        count_kept[target] = rank_kept + weight_mask[block]
        kept_of[target * CAP + rank_kept] = block
        keep = weight_mask[block].astype(jnp.float32)
        base = codes[i].astype(jnp.float32) * base_scale[block]
        values = weight[i] - base
        scale = scale_of(values)
        scales[pl.ds(block, 1), :] = scale[0:1, :]
        rounded = (values * (keep / scale)[0:1, :]).astype(jnp.bfloat16)
        coded[block] = rounded
        refreshed[i] = (base + rounded.astype(jnp.float32) * scale[0:1, :]).astype(jnp.bfloat16)

    @pl.when(step == blocks // GROUP - 1)
    def _():
        rows = row_quarter(replica)
        lane = lax.broadcasted_iota(jnp.int32, (TILE, 128), 1)

        def one(w, carry):
            tile = jnp.zeros((TILE, 128), jnp.float32)
            for k in range(CAP):
                block = kept_of[w * CAP + k]
                if k < WHOLE:
                    whole[w * WHOLE + k] = coded[block]
                else:
                    payload[slot_rows(w, k - WHOLE, BY_ROWS_WEIGHT), :] = coded[block, rows, :]
                scale = scales[pl.ds(slot_of[w * CAP + k], 1), :]
                tile = jnp.where(lane == k, jnp.broadcast_to(scale, (TILE, 128)), tile)
            payload[tile_rows(w, BY_ROWS_WEIGHT), :] = tile.astype(jnp.bfloat16)
            return carry

        lax.fori_loop(0, WRITERS, one, 0)


def cost(flops, moved):
    return pl.CostEstimate(flops=flops, bytes_accessed=moved, transcendentals=0)


def params():
    return pltpu.CompilerParams(dimension_semantics=("arbitrary",), vmem_limit_bytes=VMEM)


def moment_call(replica, writer, weight_mask, moment_mask, moment):
    blocks, width = moment.shape[0], moment.shape[1]
    shape = (WRITERS * payload_rows(BY_ROWS_MOMENT), width)
    return pl.pallas_call(
        moment_kernel,
        grid_spec=pltpu.PrefetchScalarGridSpec(
            num_scalar_prefetch=4,
            grid=(1,),
            in_specs=[pl.BlockSpec(memory_space=pl.ANY)],
            out_specs=pl.BlockSpec(shape, lambda i, *_: (0, 0)),
            scratch_shapes=[
                pltpu.VMEM(moment.shape, jnp.float32),
                pltpu.SemaphoreType.DMA((blocks // GROUP_MOMENT,)),
                pltpu.VMEM((WRITERS, 8, 128), jnp.float32),
                pltpu.VMEM((8, 128), jnp.float32),
                pltpu.SMEM((WRITERS,), jnp.int32),
            ],
        ),
        out_shape=jax.ShapeDtypeStruct(shape, jnp.bfloat16),
        compiler_params=params(),
        cost_estimate=cost(10 << 20, 12 << 20),
    )(replica, writer, weight_mask, moment_mask, moment)


def weight_call(replica, writer, weight_mask, base_scale, weight, codes):
    blocks, width = weight.shape[0], weight.shape[1]
    moving = pl.BlockSpec((GROUP, width, width), lambda i, *_: (i, 0, 0))
    payload = (WRITERS * payload_rows(BY_ROWS_WEIGHT), width)
    whole = (WRITERS * WHOLE, width, width)
    return pl.pallas_call(
        functools.partial(weight_kernel, blocks),
        grid_spec=pltpu.PrefetchScalarGridSpec(
            num_scalar_prefetch=4,
            grid=(blocks // GROUP,),
            in_specs=[moving, moving],
            out_specs=[pl.BlockSpec(payload, lambda i, *_: (0, 0)), pl.BlockSpec(whole, lambda i, *_: (0, 0, 0)), moving],
            scratch_shapes=[
                pltpu.VMEM((blocks + 1, width, width), jnp.bfloat16),
                pltpu.VMEM((blocks + 8, 128), jnp.float32),
                pltpu.SMEM((SLOTS,), jnp.int32),
                pltpu.SMEM((SLOTS,), jnp.int32),
                pltpu.SMEM((WRITERS,), jnp.int32),
                pltpu.SMEM((WRITERS,), jnp.int32),
            ],
        ),
        out_shape=[
            jax.ShapeDtypeStruct(payload, jnp.bfloat16),
            jax.ShapeDtypeStruct(whole, jnp.bfloat16),
            jax.ShapeDtypeStruct((blocks, width, width), jnp.bfloat16),
        ],
        compiler_params=params(),
        cost_estimate=cost(20 << 20, 28 << 20),
    )(replica, writer, weight_mask, base_scale, weight, codes)


HBM = pl.BlockSpec(memory_space=pltpu.HBM)
SOURCES = 8


def spread_lines(payload, by_rows, tiles, staged, spread, sems):
    copy = pltpu.make_async_copy(payload.at[:, pl.ds(by_rows * ROWS, TILE), :], tiles, sems.at[0])
    copy.start()
    copy.wait()
    line = lax.broadcasted_iota(jnp.int32, tiles.shape, 1)
    values = tiles[...].astype(jnp.float32)
    lines = [jnp.sum(jnp.where(line == i, values, 0.0), axis=1) for i in range(5)]
    for i in range(2):
        staged[i] = lines[1 + i].astype(jnp.int32)
    copy = pltpu.make_async_copy(staged, spread, sems.at[1])
    copy.start()
    copy.wait()
    return lines


def pack(by_rows, payload, held, packed, sems, advance):
    last = packed.shape[0] - 1
    steps = WRITERS // SOURCES

    def fetch(step):
        part = pl.ds(step * SOURCES, SOURCES)
        return pltpu.make_async_copy(payload.at[part], held.at[part], sems.at[step])

    for step in range(steps):
        fetch(step).start()
    yield

    def one(s, place):
        moves = advance(s)
        for k in range(by_rows):
            packed[jnp.minimum(place, last)] = held[s, pl.ds(k * ROWS, ROWS), :]
            place = place + moves[k]
        return place

    place = 0
    for step in range(steps):
        fetch(step).wait()
        place = lax.fori_loop(step * SOURCES, (step + 1) * SOURCES, one, place)
    yield


def pack_moment_kernel(half, ticket, payload, first, second, kept_w, kept_m, totals, scales, held, packed, tiles, staged, spread, sems, tile_sems):
    steps = pack(BY_ROWS_MOMENT, payload, held, packed, sems, lambda s: [spread[1, s, k] for k in range(CAP)])
    next(steps)
    lines = spread_lines(payload, BY_ROWS_MOMENT, tiles, staged, spread, tile_sems)
    next(steps)
    first[...] = packed[0:half]
    second[...] = packed[half : 2 * half]
    scales[...] = lines[0]
    kept_w[...] = lines[1].astype(jnp.int32)
    kept_m[...] = lines[2].astype(jnp.int32)
    row = lax.broadcasted_iota(jnp.int32, (8, 128), 0)
    total_w, total_m = (jnp.sum(lines[i], axis=0, keepdims=True) for i in (3, 4))
    totals[...] = jnp.where(row == 0, total_w, jnp.where(row == 1, total_m, 0.0))


def pack_moment(capacity, ticket, payload):
    width = payload.shape[-1]
    half = capacity // 2
    part = jax.ShapeDtypeStruct((half, ROWS, width), jnp.bfloat16)
    flags = jax.ShapeDtypeStruct((WRITERS, width), jnp.int32)
    return pl.pallas_call(
        functools.partial(pack_moment_kernel, half),
        in_specs=[pl.BlockSpec(memory_space=pltpu.SMEM), HBM],
        out_shape=[
            part,
            part,
            flags,
            flags,
            jax.ShapeDtypeStruct((8, width), jnp.float32),
            jax.ShapeDtypeStruct((WRITERS, width), jnp.float32),
        ],
        scratch_shapes=[
            pltpu.VMEM((WRITERS, payload_rows(BY_ROWS_MOMENT), width), jnp.bfloat16),
            pltpu.VMEM((capacity, ROWS, width), jnp.bfloat16),
            pltpu.VMEM((WRITERS, TILE, width), jnp.bfloat16),
            pltpu.VMEM((2, WRITERS, width), jnp.int32),
            pltpu.SMEM((2, WRITERS, width), jnp.int32),
            pltpu.SemaphoreType.DMA((WRITERS // SOURCES,)),
            pltpu.SemaphoreType.DMA((2,)),
        ],
        compiler_params=pltpu.CompilerParams(vmem_limit_bytes=VMEM),
        cost_estimate=cost(0, 0),
    )(ticket, payload.reshape(WRITERS, -1, width))


def pack_weight_kernel(half, kept, payload, *refs):
    first, second, scales, held, packed, sems = refs[-6:]

    def advance(s):
        found = functools.reduce(jnp.add, [kept[s, k] for k in range(CAP)])
        return [jnp.where(found > WHOLE + k, 1, 0) for k in range(BY_ROWS_WEIGHT)]

    steps = pack(BY_ROWS_WEIGHT, payload, held, packed, sems, advance)
    next(steps)
    next(steps)
    first[...] = packed[0:half]
    second[...] = packed[half : 2 * half]
    scales[...] = held[:, pl.ds(BY_ROWS_WEIGHT * ROWS, TILE), :].astype(jnp.float32)[:, 0, :]


def pack_weight(capacity, kept, payload, earlier):
    width = payload.shape[-1]
    half = capacity // 2
    part = jax.ShapeDtypeStruct((half, ROWS, width), jnp.bfloat16)
    return pl.pallas_call(
        functools.partial(pack_weight_kernel, half),
        grid_spec=pltpu.PrefetchScalarGridSpec(
            num_scalar_prefetch=1,
            grid=(1,),
            in_specs=[HBM] * (1 + len(earlier)),
            out_specs=[pl.BlockSpec(part.shape, lambda i, *_: (0, 0, 0))] * 2 + [pl.BlockSpec((WRITERS, width), lambda i, *_: (0, 0))],
            scratch_shapes=[
                pltpu.VMEM((WRITERS, payload_rows(BY_ROWS_WEIGHT), width), jnp.bfloat16),
                pltpu.VMEM((capacity, ROWS, width), jnp.bfloat16),
                pltpu.SemaphoreType.DMA((WRITERS // SOURCES,)),
            ],
        ),
        out_shape=[part, part, jax.ShapeDtypeStruct((WRITERS, width), jnp.float32)],
        compiler_params=params(),
        cost_estimate=cost(0, 0),
    )(kept, payload.reshape(WRITERS, -1, width), *earlier)


def after_kernel(*refs):
    pass


def after(values, earlier):
    return pl.pallas_call(
        after_kernel,
        in_specs=[HBM] * (1 + len(earlier)),
        out_specs=HBM,
        out_shape=jax.ShapeDtypeStruct(values.shape, values.dtype),
        input_output_aliases={0: 0},
        compiler_params=pltpu.CompilerParams(vmem_limit_bytes=VMEM),
    )(values, *earlier)


ALL_TURNS, NEAR_TURNS, FAR_TURN = (0, 1, 2, 3), (0, 1, 3), (2,)


def unpack_kernel(by_rows, half, turns, replica, kept, *refs):
    n_whole = CAP - by_rows
    n_parts = 2 * len(turns)
    parts, refs = refs[:n_parts], refs[n_parts:]
    whole = refs[0] if n_whole else None
    out, held, built, sems, out_sems = refs[-5:]
    nothing, first_whole = 2 * half, 2 * half + 1
    rows = [pl.ds(pl.multiple_of(lax.rem(replica[0] + turn, 4) * ROWS, ROWS), ROWS) for turn in turns]
    copies = [pltpu.make_async_copy(part, held.at[i // 2, pl.ds((i % 2) * half, half)], sems.at[i]) for i, part in enumerate(parts)]
    if n_whole:
        for i in range(len(turns)):
            here = held.at[i, pl.ds(first_whole, WRITERS * n_whole)]
            copies.append(pltpu.make_async_copy(whole.at[:, rows[i], :], here, sems.at[n_parts + i]))
    for copy in copies:
        copy.start()
    for i in range(len(turns)):
        held[i, nothing] = jnp.zeros(held.shape[2:], held.dtype)
    for copy in copies:
        copy.wait()

    def send(step):
        part = pl.ds(step * SOURCES * CAP, SOURCES * CAP)
        there = out.at[part, rows[0], :] if len(turns) == 1 else out.at[part]
        return pltpu.make_async_copy(built.at[part], there, out_sems.at[step])

    def one(step, place):
        for s in range(SOURCES):
            source = step * SOURCES + s
            rank = 0
            for k in range(CAP):
                flag = kept[source, k]
                if n_whole:
                    as_whole = rank < n_whole
                    origin = jnp.where(as_whole, first_whole + source * n_whole + rank, jnp.minimum(place, nothing - 1))
                    place = place + jnp.where(as_whole, 0, flag)
                    rank = rank + flag
                else:
                    origin = jnp.minimum(place, nothing - 1)
                    place = place + flag
                origin = jnp.where(flag > 0, origin, nothing)
                for i in range(len(turns)):
                    if len(turns) == 1:
                        built[source * CAP + k] = held[i, origin]
                    else:
                        built[source * CAP + k, rows[i], :] = held[i, origin]
        send(step).start()
        return place

    steps = WRITERS // SOURCES
    lax.fori_loop(0, steps, one, 0)
    for step in range(steps):
        send(step).wait()


def unpack_call(by_rows, capacity, turns, replica, kept, parts, whole=None, out=None):
    width = parts[0].shape[-1]
    n_whole = WRITERS * (CAP - by_rows)
    parts = [part for turn in turns for part in parts[2 * turn : 2 * turn + 2]]
    operands = [*parts] + ([] if whole is None else [whole]) + ([] if out is None else [out])
    return pl.pallas_call(
        functools.partial(unpack_kernel, by_rows, capacity // 2, turns),
        grid_spec=pltpu.PrefetchScalarGridSpec(
            num_scalar_prefetch=2,
            grid=(1,),
            in_specs=[HBM] * len(operands),
            out_specs=HBM,
            scratch_shapes=[
                pltpu.VMEM((len(turns), capacity + 1 + n_whole, ROWS, width), jnp.bfloat16),
                pltpu.VMEM((SLOTS, ROWS if len(turns) == 1 else width, width), jnp.bfloat16),
                pltpu.SemaphoreType.DMA((3 * len(turns),)),
                pltpu.SemaphoreType.DMA((WRITERS // SOURCES,)),
            ],
        ),
        out_shape=jax.ShapeDtypeStruct((SLOTS, width, width), jnp.bfloat16),
        input_output_aliases={} if out is None else {1 + len(operands): 0},
        compiler_params=params(),
        cost_estimate=cost(0, 0),
    )(replica, kept, *operands)


def regroup(values):
    return lax.all_to_all(values, "fsdp", split_axis=0, concat_axis=0, tiled=True)


def upward(values):
    return lax.ppermute(values, "replica", [(i, (i + 1) % 4) for i in range(4)])


def downward(values):
    return lax.ppermute(values, "replica", [(i, (i - 1) % 4) for i in range(4)])


def first_round(first, second):
    first_up, second_down = upward(first), downward(second)
    return first_up, downward(first), upward(second), second_down


def second_round(first_up, second_down):
    return upward(first_up), downward(second_down)


def by_turn(first, second, near, far):
    return (first, second, near[1], near[3], *far, near[0], near[2])


def rest(capacities, replica, m_read, m_near, m_far, w_read, w_near, w_far, w_whole):
    written_moment = unpack_call(BY_ROWS_MOMENT, capacities[0], ALL_TURNS, replica, m_read[3], by_turn(*m_read[:2], m_near, m_far))
    if w_far is None:
        w_near = (after(w_near[0], (written_moment,)), *w_near[1:3], after(w_near[3], (written_moment,)))
        w_far = second_round(w_near[0], w_near[3])
    written_weight = unpack_call(
        BY_ROWS_WEIGHT, capacities[1], ALL_TURNS, replica, m_read[2], by_turn(*w_read[:2], w_near, w_far), w_whole
    )
    return written_weight, written_moment


def exchange_again(ticket, replica, m_payload, w_payload, w_whole):
    m_read = pack_moment(FULL[0], ticket, m_payload)
    m_near = first_round(*m_read[:2])
    m_far = second_round(m_near[0], m_near[3])
    w_read = pack_weight(FULL[1], m_read[2], w_payload, ())
    w_near = first_round(*w_read[:2])
    w_far = second_round(w_near[0], w_near[3])
    return rest(FULL, replica, m_read, m_near, m_far, w_read, w_near, w_far, w_whole)


def on_device(weight, moment, base_codes, base_scale, weight_mask, moment_mask, writer):
    width = weight.shape[1]
    target = writer[:, 0]
    replica = lax.axis_index("replica").astype(jnp.int32).reshape(1)
    m_payload = regroup(moment_call(replica, target, weight_mask, moment_mask, moment))
    w_payload, w_whole, refreshed = weight_call(replica, target, weight_mask, base_scale, weight, base_codes)
    w_payload = regroup(after(w_payload, (m_payload,)))
    m_read = pack_moment(USUAL[0], replica, m_payload)
    m_near = first_round(*m_read[:2])
    m_far = second_round(m_near[0], m_near[3])
    w_read = pack_weight(USUAL[1], m_read[2], w_payload, m_near)
    w_whole = regroup(after(w_whole, (*w_read[:2], *m_far)))
    w_near = first_round(*w_read[:2])
    written_weight, written_moment = rest(USUAL, replica, m_read, m_near, m_far, w_read, w_near, None, w_whole)

    over = jnp.any(m_read[4][:2, :WRITERS] >= jnp.array([[USUAL[1]], [USUAL[0]]], jnp.float32)).astype(jnp.int32)
    _, written_weight, written_moment = lax.while_loop(
        lambda carry: carry[0] < over,
        lambda carry: (carry[0] + 1, *exchange_again(carry[0].reshape(1), replica, m_payload, w_payload, w_whole)),
        (jnp.int32(0), written_weight, written_moment),
    )
    written_scales = jnp.stack([w_read[2][:, :CAP], m_read[5][:, :CAP]], axis=0).astype(jnp.bfloat16)
    shape = (WRITERS, CAP, width, width)
    return written_weight.reshape(shape), written_moment.reshape(shape), written_scales, refreshed


def solution(mesh):
    placed = (
        P("fsdp", None, None),
        P("fsdp", None, None),
        P("fsdp", None, None),
        P("fsdp"),
        P("fsdp"),
        P("fsdp"),
        P("fsdp", None),
    )
    return jax.shard_map(
        on_device,
        mesh=mesh,
        in_specs=placed,
        out_specs=(
            P("fsdp", None, None, None),
            P("fsdp", None, None, None),
            P(None, "fsdp", None),
            P("fsdp", None, None),
        ),
        check_vma=False,
    )
```

```python
import functools

import jax
import jax.numpy as jnp
from jax import lax
from jax.experimental import pallas as pl
from jax.experimental.pallas import tpu as pltpu
from jax.sharding import PartitionSpec as P

EPSILON = 1e-06
WRITERS = 32
CAP = 8
GROUP = 8
GROUP_MOMENT = 16
ROWS = 32
TILE = 16
SLOTS = WRITERS * CAP
VMEM = 60 * 1024 * 1024

WHOLE = 3
BY_ROWS_MOMENT = CAP
BY_ROWS_WEIGHT = CAP - WHOLE
USUAL = ((54, 54), (56,))
FULL = ((132, 132), (168,))


def clear(ref, length, value):
    def one(i, carry):
        ref[i] = value
        return carry

    lax.fori_loop(0, length, one, 0, unroll=8)


def scale_of(values):
    top = jnp.max(jnp.max(jnp.abs(values), axis=0, keepdims=True), axis=1, keepdims=True)
    top = jnp.broadcast_to(top + EPSILON, (8, 128))
    return top.astype(jnp.bfloat16).astype(jnp.float32)


def row_quarter(replica):
    return pl.ds(pl.multiple_of(replica[0] * ROWS, ROWS), ROWS)


def payload_rows(by_rows):
    return by_rows * ROWS + TILE


def tile_rows(writer, by_rows):
    return pl.ds(pl.multiple_of(writer * payload_rows(by_rows) + by_rows * ROWS, TILE), TILE)


def slot_rows(writer, k, by_rows):
    return pl.ds(pl.multiple_of(writer * payload_rows(by_rows) + k * ROWS, TILE), ROWS)


def moment_kernel(replica, writer, weight_mask, moment_mask, moment, payload, held, sems, tiles, totals, count):
    rows = row_quarter(replica)
    lane = lax.broadcasted_iota(jnp.int32, (8, 128), 1)
    line = lax.broadcasted_iota(jnp.int32, (8, 128), 0)
    steps = held.shape[0] // GROUP_MOMENT

    def fetch(step):
        part = pl.ds(step * GROUP_MOMENT, GROUP_MOMENT)
        return pltpu.make_async_copy(moment.at[part], held.at[part], sems.at[step])

    for step in range(steps):
        fetch(step).start()
    clear(count, WRITERS, 0)
    tiles[...] = jnp.zeros(tiles.shape, tiles.dtype)
    totals[...] = jnp.zeros(totals.shape, totals.dtype)

    def one_step(step, carry):
        fetch(step).wait()
        total = totals[...]
        for i in range(GROUP_MOMENT):
            block = step * GROUP_MOMENT + i
            target = writer[block]
            rank = count[target]
            count[target] = rank + 1
            keep_w = weight_mask[block].astype(jnp.float32)
            keep_m = keep_w * moment_mask[block].astype(jnp.float32)
            total = total + jnp.where(lane == target, jnp.where(line == 3, keep_w, jnp.where(line == 4, keep_m, 0.0)), 0.0)
            scale = scale_of(held[block])
            kept = jnp.where(line == 0, scale, jnp.where(line == 1, keep_w, jnp.where(line == 2, keep_m, 0.0)))
            tiles[target] = jnp.where(lane == rank, kept, tiles[target])
            payload[slot_rows(target, rank, BY_ROWS_MOMENT), :] = (held[block, rows, :] * (keep_m / scale)[0:1, :]).astype(jnp.bfloat16)
        totals[...] = total
        return carry

    lax.fori_loop(0, steps, one_step, 0)
    common = totals[...]
    common = jnp.where(line == 3, jnp.maximum(common - WHOLE, 0.0), common)
    blank = jnp.zeros((TILE - 8, 128), jnp.float32)

    def one(w, carry):
        tile = jnp.concatenate([tiles[w] + common, blank], axis=0)
        payload[tile_rows(w, BY_ROWS_MOMENT), :] = tile.astype(jnp.bfloat16)
        return carry

    lax.fori_loop(0, WRITERS, one, 0, unroll=4)


def weight_kernel(blocks, replica, writer, weight_mask, base_scale, weight, codes, payload, whole, refreshed, coded, scales, slot_of, kept_of, count, count_kept):
    step = pl.program_id(0)

    @pl.when(step == 0)
    def _():
        clear(slot_of, SLOTS, blocks)
        clear(kept_of, SLOTS, blocks)
        clear(count, WRITERS, 0)
        clear(count_kept, WRITERS, 0)
        coded[blocks] = jnp.zeros(coded.shape[1:], coded.dtype)
        scales[pl.ds(blocks, 8), :] = jnp.zeros((8, 128), jnp.float32)

    for i in range(GROUP):
        block = step * GROUP + i
        target = writer[block]
        rank = count[target]
        count[target] = rank + 1
        slot_of[target * CAP + rank] = block
        rank_kept = count_kept[target]
        count_kept[target] = rank_kept + weight_mask[block]
        kept_of[target * CAP + rank_kept] = block
        keep = weight_mask[block].astype(jnp.float32)
        base = codes[i].astype(jnp.float32) * base_scale[block]
        values = weight[i] - base
        scale = scale_of(values)
        scales[pl.ds(block, 1), :] = scale[0:1, :]
        rounded = (values * (keep / scale)[0:1, :]).astype(jnp.bfloat16)
        coded[block] = rounded
        refreshed[i] = (base + rounded.astype(jnp.float32) * scale[0:1, :]).astype(jnp.bfloat16)

    @pl.when(step == blocks // GROUP - 1)
    def _():
        rows = row_quarter(replica)
        lane = lax.broadcasted_iota(jnp.int32, (TILE, 128), 1)

        def one(w, carry):
            tile = jnp.zeros((TILE, 128), jnp.float32)
            for k in range(CAP):
                block = kept_of[w * CAP + k]
                if k < WHOLE:
                    whole[w * WHOLE + k] = coded[block]
                else:
                    payload[slot_rows(w, k - WHOLE, BY_ROWS_WEIGHT), :] = coded[block, rows, :]
                scale = scales[pl.ds(slot_of[w * CAP + k], 1), :]
                tile = jnp.where(lane == k, jnp.broadcast_to(scale, (TILE, 128)), tile)
            payload[tile_rows(w, BY_ROWS_WEIGHT), :] = tile.astype(jnp.bfloat16)
            return carry

        lax.fori_loop(0, WRITERS, one, 0)


def cost(flops, moved):
    return pl.CostEstimate(flops=flops, bytes_accessed=moved, transcendentals=0)


def params():
    return pltpu.CompilerParams(dimension_semantics=("arbitrary",), vmem_limit_bytes=VMEM)


def moment_call(replica, writer, weight_mask, moment_mask, moment):
    blocks, width = moment.shape[0], moment.shape[1]
    shape = (WRITERS * payload_rows(BY_ROWS_MOMENT), width)
    return pl.pallas_call(
        moment_kernel,
        grid_spec=pltpu.PrefetchScalarGridSpec(
            num_scalar_prefetch=4,
            grid=(1,),
            in_specs=[pl.BlockSpec(memory_space=pl.ANY)],
            out_specs=pl.BlockSpec(shape, lambda i, *_: (0, 0)),
            scratch_shapes=[
                pltpu.VMEM(moment.shape, jnp.float32),
                pltpu.SemaphoreType.DMA((blocks // GROUP_MOMENT,)),
                pltpu.VMEM((WRITERS, 8, 128), jnp.float32),
                pltpu.VMEM((8, 128), jnp.float32),
                pltpu.SMEM((WRITERS,), jnp.int32),
            ],
        ),
        out_shape=jax.ShapeDtypeStruct(shape, jnp.bfloat16),
        compiler_params=params(),
        cost_estimate=cost(10 << 20, 12 << 20),
    )(replica, writer, weight_mask, moment_mask, moment)


def weight_call(replica, writer, weight_mask, base_scale, weight, codes):
    blocks, width = weight.shape[0], weight.shape[1]
    moving = pl.BlockSpec((GROUP, width, width), lambda i, *_: (i, 0, 0))
    payload = (WRITERS * payload_rows(BY_ROWS_WEIGHT), width)
    whole = (WRITERS * WHOLE, width, width)
    return pl.pallas_call(
        functools.partial(weight_kernel, blocks),
        grid_spec=pltpu.PrefetchScalarGridSpec(
            num_scalar_prefetch=4,
            grid=(blocks // GROUP,),
            in_specs=[moving, moving],
            out_specs=[pl.BlockSpec(payload, lambda i, *_: (0, 0)), pl.BlockSpec(whole, lambda i, *_: (0, 0, 0)), moving],
            scratch_shapes=[
                pltpu.VMEM((blocks + 1, width, width), jnp.bfloat16),
                pltpu.VMEM((blocks + 8, 128), jnp.float32),
                pltpu.SMEM((SLOTS,), jnp.int32),
                pltpu.SMEM((SLOTS,), jnp.int32),
                pltpu.SMEM((WRITERS,), jnp.int32),
                pltpu.SMEM((WRITERS,), jnp.int32),
            ],
        ),
        out_shape=[
            jax.ShapeDtypeStruct(payload, jnp.bfloat16),
            jax.ShapeDtypeStruct(whole, jnp.bfloat16),
            jax.ShapeDtypeStruct((blocks, width, width), jnp.bfloat16),
        ],
        compiler_params=params(),
        cost_estimate=cost(20 << 20, 28 << 20),
    )(replica, writer, weight_mask, base_scale, weight, codes)


HBM = pl.BlockSpec(memory_space=pltpu.HBM)
SOURCES = 8


def spread_lines(payload, by_rows, tiles, staged, spread, sems):
    copy = pltpu.make_async_copy(payload.at[:, pl.ds(by_rows * ROWS, TILE), :], tiles, sems.at[0])
    copy.start()
    copy.wait()
    line = lax.broadcasted_iota(jnp.int32, tiles.shape, 1)
    values = tiles[...].astype(jnp.float32)
    lines = [jnp.sum(jnp.where(line == i, values, 0.0), axis=1) for i in range(5)]
    for i in range(2):
        staged[i] = lines[1 + i].astype(jnp.int32)
    copy = pltpu.make_async_copy(staged, spread, sems.at[1])
    copy.start()
    copy.wait()
    return lines


def pack(by_rows, payload, held, packed, sems, advance):
    last = packed.shape[0] - 1
    steps = WRITERS // SOURCES

    def fetch(step):
        part = pl.ds(step * SOURCES, SOURCES)
        return pltpu.make_async_copy(payload.at[part], held.at[part], sems.at[step])

    for step in range(steps):
        fetch(step).start()
    yield

    def one(s, place):
        moves = advance(s)
        for k in range(by_rows):
            packed[jnp.minimum(place, last)] = held[s, pl.ds(k * ROWS, ROWS), :]
            place = place + moves[k]
        return place

    place = 0
    for step in range(steps):
        fetch(step).wait()
        place = lax.fori_loop(step * SOURCES, (step + 1) * SOURCES, one, place)
    yield


def share(packed, own):
    start = 0
    for part in own:
        part[...] = packed[start : start + part.shape[0]]
        start += part.shape[0]


def pack_moment_kernel(ticket, payload, *refs):
    *own, kept_w, kept_m, totals, scales, held, packed, tiles, staged, spread, sems, tile_sems = refs
    steps = pack(BY_ROWS_MOMENT, payload, held, packed, sems, lambda s: [spread[1, s, k] for k in range(CAP)])
    next(steps)
    lines = spread_lines(payload, BY_ROWS_MOMENT, tiles, staged, spread, tile_sems)
    next(steps)
    share(packed, own)
    scales[...] = lines[0]
    kept_w[...] = lines[1].astype(jnp.int32)
    kept_m[...] = lines[2].astype(jnp.int32)
    row = lax.broadcasted_iota(jnp.int32, (8, 128), 0)
    total_w, total_m = (jnp.sum(lines[i], axis=0, keepdims=True) for i in (3, 4))
    totals[...] = jnp.where(row == 0, total_w, jnp.where(row == 1, total_m, 0.0))


def pack_moment(capacity, ticket, payload):
    width = payload.shape[-1]
    parts = [jax.ShapeDtypeStruct((size, ROWS, width), jnp.bfloat16) for size in capacity]
    flags = jax.ShapeDtypeStruct((WRITERS, width), jnp.int32)
    return pl.pallas_call(
        pack_moment_kernel,
        in_specs=[pl.BlockSpec(memory_space=pltpu.SMEM), HBM],
        out_shape=[
            *parts,
            flags,
            flags,
            jax.ShapeDtypeStruct((8, width), jnp.float32),
            jax.ShapeDtypeStruct((WRITERS, width), jnp.float32),
        ],
        scratch_shapes=[
            pltpu.VMEM((WRITERS, payload_rows(BY_ROWS_MOMENT), width), jnp.bfloat16),
            pltpu.VMEM((sum(capacity), ROWS, width), jnp.bfloat16),
            pltpu.VMEM((WRITERS, TILE, width), jnp.bfloat16),
            pltpu.VMEM((2, WRITERS, width), jnp.int32),
            pltpu.SMEM((2, WRITERS, width), jnp.int32),
            pltpu.SemaphoreType.DMA((WRITERS // SOURCES,)),
            pltpu.SemaphoreType.DMA((2,)),
        ],
        compiler_params=pltpu.CompilerParams(vmem_limit_bytes=VMEM),
        cost_estimate=cost(0, 0),
    )(ticket, payload.reshape(WRITERS, -1, width))


def pack_weight_kernel(kept, payload, *refs):
    *own, scales, held, packed, sems = refs

    def advance(s):
        found = functools.reduce(jnp.add, [kept[s, k] for k in range(CAP)])
        return [jnp.where(found > WHOLE + k, 1, 0) for k in range(BY_ROWS_WEIGHT)]

    steps = pack(BY_ROWS_WEIGHT, payload, held, packed, sems, advance)
    next(steps)
    next(steps)
    share(packed, own)
    scales[...] = held[:, pl.ds(BY_ROWS_WEIGHT * ROWS, TILE), :].astype(jnp.float32)[:, 0, :]


def pack_weight(capacity, kept, payload):
    width = payload.shape[-1]
    parts = [jax.ShapeDtypeStruct((size, ROWS, width), jnp.bfloat16) for size in capacity]
    return pl.pallas_call(
        pack_weight_kernel,
        grid_spec=pltpu.PrefetchScalarGridSpec(
            num_scalar_prefetch=1,
            grid=(1,),
            in_specs=[HBM],
            out_specs=[pl.BlockSpec(part.shape, lambda i, *_: (0, 0, 0)) for part in parts] + [pl.BlockSpec((WRITERS, width), lambda i, *_: (0, 0))],
            scratch_shapes=[
                pltpu.VMEM((WRITERS, payload_rows(BY_ROWS_WEIGHT), width), jnp.bfloat16),
                pltpu.VMEM((sum(capacity), ROWS, width), jnp.bfloat16),
                pltpu.SemaphoreType.DMA((WRITERS // SOURCES,)),
            ],
        ),
        out_shape=[*parts, jax.ShapeDtypeStruct((WRITERS, width), jnp.float32)],
        compiler_params=params(),
        cost_estimate=cost(0, 0),
    )(kept, payload.reshape(WRITERS, -1, width))


def after_kernel(*refs):
    pass


def after(values, earlier):
    return pl.pallas_call(
        after_kernel,
        in_specs=[HBM] * (1 + len(earlier)),
        out_specs=HBM,
        out_shape=jax.ShapeDtypeStruct(values.shape, values.dtype),
        input_output_aliases={0: 0},
        compiler_params=pltpu.CompilerParams(vmem_limit_bytes=VMEM),
    )(values, *earlier)


def unpack_kernel(n_whole, sizes, replica, kept, *refs):
    out, held, built, sems, out_sems = refs[-5:]
    nothing = sum(sizes[0])
    first_whole = nothing + 1
    rows = [pl.ds(pl.multiple_of(lax.rem(replica[0] + turn, 4) * ROWS, ROWS), ROWS) for turn in range(4)]
    copies = []
    for turn in range(4):
        start = 0
        for size in sizes[turn]:
            i = len(copies)
            copies.append(pltpu.make_async_copy(refs[i], held.at[turn, pl.ds(start, size)], sems.at[i]))
            start += size
    if n_whole:
        whole = refs[len(copies)]
        for turn in range(4):
            there = held.at[turn, pl.ds(first_whole, WRITERS * n_whole)]
            copies.append(pltpu.make_async_copy(whole.at[:, rows[turn], :], there, sems.at[len(copies)]))
    for copy in copies:
        copy.start()
    for turn in range(4):
        held[turn, nothing] = jnp.zeros(held.shape[2:], held.dtype)
    for copy in copies:
        copy.wait()

    def send(step):
        part = pl.ds(step * SOURCES * CAP, SOURCES * CAP)
        return pltpu.make_async_copy(built.at[part], out.at[part], out_sems.at[step])

    def one(step, place):
        for s in range(SOURCES):
            source = step * SOURCES + s
            rank = 0
            for k in range(CAP):
                flag = kept[source, k]
                origin = jnp.minimum(place, nothing - 1)
                if n_whole:
                    as_whole = rank < n_whole
                    origin = jnp.where(as_whole, first_whole + source * n_whole + rank, origin)
                    place = place + jnp.where(as_whole, 0, flag)
                    rank = rank + flag
                else:
                    place = place + flag
                origin = jnp.where(flag > 0, origin, nothing)
                for turn in range(4):
                    built[source * CAP + k, rows[turn], :] = held[turn, origin]
        send(step).start()
        return place

    steps = WRITERS // SOURCES
    lax.fori_loop(0, steps, one, 0)
    for step in range(steps):
        send(step).wait()


def unpack(replica, kept, parts, whole=None):
    sizes = [[piece.shape[0] for piece in part] for part in parts]
    operands = [piece for part in parts for piece in part] + ([] if whole is None else [whole])
    n_whole = 0 if whole is None else WHOLE
    width = operands[0].shape[-1]
    return pl.pallas_call(
        functools.partial(unpack_kernel, n_whole, sizes),
        grid_spec=pltpu.PrefetchScalarGridSpec(
            num_scalar_prefetch=2,
            grid=(1,),
            in_specs=[HBM] * len(operands),
            out_specs=HBM,
            scratch_shapes=[
                pltpu.VMEM((4, sum(sizes[0]) + 1 + WRITERS * n_whole, ROWS, width), jnp.bfloat16),
                pltpu.VMEM((SLOTS, width, width), jnp.bfloat16),
                pltpu.SemaphoreType.DMA((len(operands) + 4,)),
                pltpu.SemaphoreType.DMA((WRITERS // SOURCES,)),
            ],
        ),
        out_shape=jax.ShapeDtypeStruct((SLOTS, width, width), jnp.bfloat16),
        compiler_params=params(),
        cost_estimate=cost(0, 0),
    )(replica, kept, *operands)


def regroup(values):
    return lax.all_to_all(values, "fsdp", split_axis=0, concat_axis=0, tiled=True)


def upward(values):
    return lax.ppermute(values, "replica", [(i, (i + 1) % 4) for i in range(4)])


def downward(values):
    return lax.ppermute(values, "replica", [(i, (i - 1) % 4) for i in range(4)])


def along_z(first, second):
    first_up, first_down = upward(first), downward(first)
    second_up, second_down = upward(second), downward(second)
    return (first_up, second_down), ((first, second), (first_down, second_down), (upward(first_up), downward(second_down)), (first_up, second_up))


def along_z_down(own):
    up, down = upward(own), downward(own)
    return ((own,), (down,), (downward(down),), (up,))


def exchange_again(ticket, replica, m_payload, w_payload, w_whole):
    *m_own, kept_w, kept_m, _, _ = pack_moment(FULL[0], ticket, m_payload)
    written_moment = unpack(replica, kept_m, along_z(*m_own)[1])
    *w_own, _ = pack_weight(FULL[1], kept_w, w_payload)
    written_weight = unpack(replica, kept_w, along_z_down(*w_own), w_whole)
    return written_weight, written_moment


def on_device(weight, moment, base_codes, base_scale, weight_mask, moment_mask, writer):
    width = weight.shape[1]
    target = writer[:, 0]
    replica = lax.axis_index("replica").astype(jnp.int32).reshape(1)
    m_payload = regroup(moment_call(replica, target, weight_mask, moment_mask, moment))
    w_payload, w_whole, refreshed = weight_call(replica, target, weight_mask, base_scale, weight, base_codes)
    w_payload = regroup(after(w_payload, (m_payload,)))
    *m_own, kept_w, kept_m, totals, m_scales = pack_moment(USUAL[0], replica, m_payload)
    m_near, m_parts = along_z(*m_own)
    w_whole = regroup(after(w_whole, (w_payload, *m_near)))
    *w_own, w_scales = pack_weight(USUAL[1], kept_w, w_payload)
    w_parts = along_z_down(*w_own)
    written_moment = unpack(replica, kept_m, m_parts)
    written_weight = unpack(replica, kept_w, w_parts, w_whole)

    over = jnp.any(totals[:2, :WRITERS] >= jnp.array([[sum(USUAL[1])], [sum(USUAL[0])]], jnp.float32)).astype(jnp.int32)
    _, written_weight, written_moment = lax.while_loop(
        lambda carry: carry[0] < over,
        lambda carry: (carry[0] + 1, *exchange_again(carry[0].reshape(1), replica, m_payload, w_payload, w_whole)),
        (jnp.int32(0), written_weight, written_moment),
    )
    written_scales = jnp.stack([w_scales[:, :CAP], m_scales[:, :CAP]], axis=0).astype(jnp.bfloat16)
    shape = (WRITERS, CAP, width, width)
    return written_weight.reshape(shape), written_moment.reshape(shape), written_scales, refreshed


def solution(mesh):
    placed = (
        P("fsdp", None, None),
        P("fsdp", None, None),
        P("fsdp", None, None),
        P("fsdp"),
        P("fsdp"),
        P("fsdp"),
        P("fsdp", None),
    )
    return jax.shard_map(
        on_device,
        mesh=mesh,
        in_specs=placed,
        out_specs=(
            P("fsdp", None, None, None),
            P("fsdp", None, None, None),
            P(None, "fsdp", None),
            P("fsdp", None, None),
        ),
        check_vma=False,
    )
```

```python
import functools

import jax
import jax.numpy as jnp
from jax import lax
from jax.experimental import pallas as pl
from jax.experimental.pallas import tpu as pltpu
from jax.sharding import PartitionSpec as P

EPSILON = 1e-06
WRITERS = 32
CAP = 8
GROUP = 8
GROUP_MOMENT = 16
ROWS = 32
TILE = 16
SLOTS = WRITERS * CAP
VMEM = 60 * 1024 * 1024
HBM = pl.BlockSpec(memory_space=pltpu.HBM)

WHOLE = 3
BY_ROWS_MOMENT = CAP
BY_ROWS_WEIGHT = CAP - WHOLE
USUAL = ((54, 54), (28, 28))
FULL = ((132, 132), (84, 84))


def clear(ref, length, value):
    def one(i, carry):
        ref[i] = value
        return carry

    lax.fori_loop(0, length, one, 0, unroll=8)


def scale_of(values):
    top = jnp.max(jnp.max(jnp.abs(values), axis=0, keepdims=True), axis=1, keepdims=True)
    top = jnp.broadcast_to(top + EPSILON, (8, 128))
    return top.astype(jnp.bfloat16).astype(jnp.float32)


def row_quarter():
    return pl.ds(pl.multiple_of(lax.axis_index("replica") * ROWS, ROWS), ROWS)


def payload_rows(by_rows):
    return by_rows * ROWS + TILE


def tile_rows(writer, by_rows):
    return pl.ds(pl.multiple_of(writer * payload_rows(by_rows) + by_rows * ROWS, TILE), TILE)


def slot_rows(writer, k, by_rows):
    return pl.ds(pl.multiple_of(writer * payload_rows(by_rows) + k * ROWS, TILE), ROWS)


def moment_kernel(
    writer_in, weight_mask_in, moment_mask_in, moment, payload, held, sems, tiles, totals, count, writer, weight_mask, moment_mask, scalar_sems
):
    rows = row_quarter()
    lane = lax.broadcasted_iota(jnp.int32, (8, 128), 1)
    line = lax.broadcasted_iota(jnp.int32, (8, 128), 0)
    steps = held.shape[0] // GROUP_MOMENT

    def fetch(step):
        part = pl.ds(step * GROUP_MOMENT, GROUP_MOMENT)
        return pltpu.make_async_copy(moment.at[part], held.at[part], sems.at[step])

    scalars = ((writer_in, writer), (weight_mask_in, weight_mask), (moment_mask_in, moment_mask))
    scalars = [pltpu.make_async_copy(source, there, scalar_sems.at[i]) for i, (source, there) in enumerate(scalars)]
    for copy in scalars:
        copy.start()
    for step in range(steps):
        fetch(step).start()
    clear(count, WRITERS, 0)
    tiles[...] = jnp.zeros(tiles.shape, tiles.dtype)
    totals[...] = jnp.zeros(totals.shape, totals.dtype)
    for copy in scalars:
        copy.wait()

    def one_step(step, carry):
        fetch(step).wait()
        total = totals[...]
        for i in range(GROUP_MOMENT):
            block = step * GROUP_MOMENT + i
            target = writer[block]
            rank = count[target]
            count[target] = rank + 1
            keep_w = weight_mask[block].astype(jnp.float32)
            keep_m = keep_w * moment_mask[block].astype(jnp.float32)
            total = total + jnp.where(lane == target, jnp.where(line == 3, keep_w, jnp.where(line == 4, keep_m, 0.0)), 0.0)
            scale = scale_of(held[block])
            kept = jnp.where(line == 0, scale, jnp.where(line == 1, keep_w, jnp.where(line == 2, keep_m, 0.0)))
            tiles[target] = jnp.where(lane == rank, kept, tiles[target])
            payload[slot_rows(target, rank, BY_ROWS_MOMENT), :] = (held[block, rows, :] * (keep_m / scale)[0:1, :]).astype(jnp.bfloat16)
        totals[...] = total
        return carry

    lax.fori_loop(0, steps, one_step, 0)
    common = totals[...]
    common = jnp.where(line == 3, jnp.maximum(common - WHOLE, 0.0), common)
    blank = jnp.zeros((TILE - 8, 128), jnp.float32)

    def one(w, carry):
        tile = jnp.concatenate([tiles[w] + common, blank], axis=0)
        payload[tile_rows(w, BY_ROWS_MOMENT), :] = tile.astype(jnp.bfloat16)
        return carry

    lax.fori_loop(0, WRITERS, one, 0, unroll=4)


def weight_kernel(blocks, writer, weight_mask, base_scale, weight, codes, payload, whole, refreshed, coded, scales, slot_of, kept_of, count, count_kept):
    step = pl.program_id(0)

    @pl.when(step == 0)
    def _():
        clear(slot_of, SLOTS, blocks)
        clear(kept_of, SLOTS, blocks)
        clear(count, WRITERS, 0)
        clear(count_kept, WRITERS, 0)
        coded[blocks] = jnp.zeros(coded.shape[1:], coded.dtype)
        scales[pl.ds(blocks, 8), :] = jnp.zeros((8, 128), jnp.float32)

    for i in range(GROUP):
        block = step * GROUP + i
        target = writer[block]
        rank = count[target]
        count[target] = rank + 1
        slot_of[target * CAP + rank] = block
        rank_kept = count_kept[target]
        count_kept[target] = rank_kept + weight_mask[block]
        kept_of[target * CAP + rank_kept] = block
        keep = weight_mask[block].astype(jnp.float32)
        base = codes[i].astype(jnp.float32) * base_scale[block]
        values = weight[i] - base
        scale = scale_of(values)
        scales[pl.ds(block, 1), :] = scale[0:1, :]
        rounded = (values * (keep / scale)[0:1, :]).astype(jnp.bfloat16)
        coded[block] = rounded
        refreshed[i] = (base + rounded.astype(jnp.float32) * scale[0:1, :]).astype(jnp.bfloat16)

    @pl.when(step == blocks // GROUP - 1)
    def _():
        rows = row_quarter()
        lane = lax.broadcasted_iota(jnp.int32, (TILE, 128), 1)

        def one(w, carry):
            tile = jnp.zeros((TILE, 128), jnp.float32)
            for k in range(CAP):
                block = kept_of[w * CAP + k]
                if k < WHOLE:
                    whole[w * WHOLE + k] = coded[block]
                else:
                    payload[slot_rows(w, k - WHOLE, BY_ROWS_WEIGHT), :] = coded[block, rows, :]
                scale = scales[pl.ds(slot_of[w * CAP + k], 1), :]
                tile = jnp.where(lane == k, jnp.broadcast_to(scale, (TILE, 128)), tile)
            payload[tile_rows(w, BY_ROWS_WEIGHT), :] = tile.astype(jnp.bfloat16)
            return carry

        lax.fori_loop(0, WRITERS, one, 0)


def cost(flops, moved):
    return pl.CostEstimate(flops=flops, bytes_accessed=moved, transcendentals=0)


def params():
    return pltpu.CompilerParams(dimension_semantics=("arbitrary",), vmem_limit_bytes=VMEM)


def moment_call(writer, weight_mask, moment_mask, moment):
    blocks, width = moment.shape[0], moment.shape[1]
    shape = (WRITERS * payload_rows(BY_ROWS_MOMENT), width)
    return pl.pallas_call(
        moment_kernel,
        in_specs=[HBM] * 4,
        out_shape=jax.ShapeDtypeStruct(shape, jnp.bfloat16),
        scratch_shapes=[
            pltpu.VMEM(moment.shape, jnp.float32),
            pltpu.SemaphoreType.DMA((blocks // GROUP_MOMENT,)),
            pltpu.VMEM((WRITERS, 8, 128), jnp.float32),
            pltpu.VMEM((8, 128), jnp.float32),
            pltpu.SMEM((WRITERS,), jnp.int32),
            pltpu.SMEM((blocks,), jnp.int32),
            pltpu.SMEM((blocks,), jnp.int32),
            pltpu.SMEM((blocks,), jnp.int32),
            pltpu.SemaphoreType.DMA((3,)),
        ],
        compiler_params=pltpu.CompilerParams(vmem_limit_bytes=VMEM),
        cost_estimate=cost(10 << 20, 12 << 20),
    )(writer, weight_mask, moment_mask, moment)


def weight_call(writer, weight_mask, base_scale, weight, codes):
    blocks, width = weight.shape[0], weight.shape[1]
    moving = pl.BlockSpec((GROUP, width, width), lambda i, *_: (i, 0, 0))
    payload = (WRITERS * payload_rows(BY_ROWS_WEIGHT), width)
    whole = (WRITERS * WHOLE, width, width)
    return pl.pallas_call(
        functools.partial(weight_kernel, blocks),
        grid_spec=pltpu.PrefetchScalarGridSpec(
            num_scalar_prefetch=3,
            grid=(blocks // GROUP,),
            in_specs=[moving, moving],
            out_specs=[pl.BlockSpec(payload, lambda i, *_: (0, 0)), pl.BlockSpec(whole, lambda i, *_: (0, 0, 0)), moving],
            scratch_shapes=[
                pltpu.VMEM((blocks + 1, width, width), jnp.bfloat16),
                pltpu.VMEM((blocks + 8, 128), jnp.float32),
                pltpu.SMEM((SLOTS,), jnp.int32),
                pltpu.SMEM((SLOTS,), jnp.int32),
                pltpu.SMEM((WRITERS,), jnp.int32),
                pltpu.SMEM((WRITERS,), jnp.int32),
            ],
        ),
        out_shape=[
            jax.ShapeDtypeStruct(payload, jnp.bfloat16),
            jax.ShapeDtypeStruct(whole, jnp.bfloat16),
            jax.ShapeDtypeStruct((blocks, width, width), jnp.bfloat16),
        ],
        compiler_params=params(),
        cost_estimate=cost(20 << 20, 28 << 20),
    )(writer, weight_mask, base_scale, weight, codes)


SOURCES = 8


def spread_lines(payload, by_rows, tiles, staged, spread, sems):
    copy = pltpu.make_async_copy(payload.at[:, pl.ds(by_rows * ROWS, TILE), :], tiles, sems.at[0])
    copy.start()
    copy.wait()
    line = lax.broadcasted_iota(jnp.int32, tiles.shape, 1)
    values = tiles[...].astype(jnp.float32)
    lines = [jnp.sum(jnp.where(line == i, values, 0.0), axis=1) for i in range(5)]
    for i in range(2):
        staged[i] = lines[1 + i].astype(jnp.int32)
    copy = pltpu.make_async_copy(staged, spread, sems.at[1])
    copy.start()
    copy.wait()
    return lines


def pack(by_rows, payload, held, packed, sems, advance):
    last = packed.shape[0] - 1
    steps = WRITERS // SOURCES

    def fetch(step):
        part = pl.ds(step * SOURCES, SOURCES)
        return pltpu.make_async_copy(payload.at[part], held.at[part], sems.at[step])

    for step in range(steps):
        fetch(step).start()
    yield

    def one(s, place):
        moves = advance(s)
        for k in range(by_rows):
            packed[jnp.minimum(place, last)] = held[s, pl.ds(k * ROWS, ROWS), :]
            place = place + moves[k]
        return place

    place = 0
    for step in range(steps):
        fetch(step).wait()
        place = lax.fori_loop(step * SOURCES, (step + 1) * SOURCES, one, place)
    yield


def share(packed, own):
    start = 0
    for part in own:
        part[...] = packed[start : start + part.shape[0]]
        start += part.shape[0]


def pack_moment_kernel(ticket, payload, *refs):
    *own, kept_w, kept_m, totals, scales, held, packed, tiles, staged, spread, sems, tile_sems = refs
    steps = pack(BY_ROWS_MOMENT, payload, held, packed, sems, lambda s: [spread[1, s, k] for k in range(CAP)])
    next(steps)
    lines = spread_lines(payload, BY_ROWS_MOMENT, tiles, staged, spread, tile_sems)
    next(steps)
    share(packed, own)
    scales[...] = lines[0]
    kept_w[...] = lines[1].astype(jnp.int32)
    kept_m[...] = lines[2].astype(jnp.int32)
    row = lax.broadcasted_iota(jnp.int32, (8, 128), 0)
    total_w, total_m = (jnp.sum(lines[i], axis=0, keepdims=True) for i in (3, 4))
    totals[...] = jnp.where(row == 0, total_w, jnp.where(row == 1, total_m, 0.0))


def pack_moment(capacity, ticket, payload):
    width = payload.shape[-1]
    parts = [jax.ShapeDtypeStruct((size, ROWS, width), jnp.bfloat16) for size in capacity]
    flags = jax.ShapeDtypeStruct((WRITERS, width), jnp.int32)
    return pl.pallas_call(
        pack_moment_kernel,
        in_specs=[HBM, HBM],
        out_shape=[
            *parts,
            flags,
            flags,
            jax.ShapeDtypeStruct((8, width), jnp.float32),
            jax.ShapeDtypeStruct((WRITERS, width), jnp.float32),
        ],
        scratch_shapes=[
            pltpu.VMEM((WRITERS, payload_rows(BY_ROWS_MOMENT), width), jnp.bfloat16),
            pltpu.VMEM((sum(capacity), ROWS, width), jnp.bfloat16),
            pltpu.VMEM((WRITERS, TILE, width), jnp.bfloat16),
            pltpu.VMEM((2, WRITERS, width), jnp.int32),
            pltpu.SMEM((2, WRITERS, width), jnp.int32),
            pltpu.SemaphoreType.DMA((WRITERS // SOURCES,)),
            pltpu.SemaphoreType.DMA((2,)),
        ],
        compiler_params=pltpu.CompilerParams(vmem_limit_bytes=VMEM),
        cost_estimate=cost(0, 0),
    )(ticket, payload.reshape(WRITERS, -1, width))


def pack_weight_kernel(kept_in, payload, *refs):
    *own, scales, held, packed, sems, kept, kept_sem = refs
    copy = pltpu.make_async_copy(kept_in, kept, kept_sem)
    copy.start()

    def advance(s):
        found = functools.reduce(jnp.add, [kept[s, k] for k in range(CAP)])
        return [jnp.where(found > WHOLE + k, 1, 0) for k in range(BY_ROWS_WEIGHT)]

    steps = pack(BY_ROWS_WEIGHT, payload, held, packed, sems, advance)
    next(steps)
    copy.wait()
    next(steps)
    share(packed, own)
    scales[...] = held[:, pl.ds(BY_ROWS_WEIGHT * ROWS, TILE), :].astype(jnp.float32)[:, 0, :]


def pack_weight(capacity, kept, payload):
    width = payload.shape[-1]
    parts = [jax.ShapeDtypeStruct((size, ROWS, width), jnp.bfloat16) for size in capacity]
    return pl.pallas_call(
        pack_weight_kernel,
        in_specs=[HBM, HBM],
        out_shape=[*parts, jax.ShapeDtypeStruct((WRITERS, width), jnp.float32)],
        scratch_shapes=[
            pltpu.VMEM((WRITERS, payload_rows(BY_ROWS_WEIGHT), width), jnp.bfloat16),
            pltpu.VMEM((sum(capacity), ROWS, width), jnp.bfloat16),
            pltpu.SemaphoreType.DMA((WRITERS // SOURCES,)),
            pltpu.SMEM(kept.shape, jnp.int32),
            pltpu.SemaphoreType.DMA,
        ],
        compiler_params=pltpu.CompilerParams(vmem_limit_bytes=VMEM),
        cost_estimate=cost(0, 0),
    )(kept, payload.reshape(WRITERS, -1, width))


def after_kernel(*refs):
    pass


def after(values, earlier):
    return pl.pallas_call(
        after_kernel,
        in_specs=[HBM] * (1 + len(earlier)),
        out_specs=HBM,
        out_shape=jax.ShapeDtypeStruct(values.shape, values.dtype),
        input_output_aliases={0: 0},
        compiler_params=pltpu.CompilerParams(vmem_limit_bytes=VMEM),
    )(values, *earlier)


def unpack_kernel(n_whole, sizes, kept_in, *refs):
    out, held, built, sems, out_sems, kept, kept_sem = refs[-7:]
    replica = lax.axis_index("replica")
    copy_kept = pltpu.make_async_copy(kept_in, kept, kept_sem)
    copy_kept.start()
    nothing = sum(sizes[0])
    first_whole = nothing + 1
    rows = [pl.ds(pl.multiple_of(lax.rem(replica + turn, 4) * ROWS, ROWS), ROWS) for turn in range(4)]
    copies = []
    for turn in range(4):
        start = 0
        for size in sizes[turn]:
            i = len(copies)
            copies.append(pltpu.make_async_copy(refs[i], held.at[turn, pl.ds(start, size)], sems.at[i]))
            start += size
    whole = refs[len(copies)] if n_whole else None

    def fetch_whole(step, turn):
        size = SOURCES * n_whole
        there = held.at[turn, pl.ds(first_whole + step * size, size)]
        return pltpu.make_async_copy(whole.at[pl.ds(step * size, size), rows[turn], :], there, sems.at[len(copies) + 4 * step + turn])

    for copy in copies:
        copy.start()
    if n_whole:
        for step in range(WRITERS // SOURCES):
            for turn in range(4):
                fetch_whole(step, turn).start()
    for turn in range(4):
        held[turn, nothing] = jnp.zeros(held.shape[2:], held.dtype)
    copy_kept.wait()
    for copy in copies:
        copy.wait()

    def send(step):
        part = pl.ds(step * SOURCES * CAP, SOURCES * CAP)
        return pltpu.make_async_copy(built.at[part], out.at[part], out_sems.at[step])

    def one(step, place):
        if n_whole:
            for turn in range(4):
                fetch_whole(step, turn).wait()
        for s in range(SOURCES):
            source = step * SOURCES + s
            rank = 0
            for k in range(CAP):
                flag = kept[source, k]
                origin = jnp.minimum(place, nothing - 1)
                if n_whole:
                    as_whole = rank < n_whole
                    origin = jnp.where(as_whole, first_whole + source * n_whole + rank, origin)
                    place = place + jnp.where(as_whole, 0, flag)
                    rank = rank + flag
                else:
                    place = place + flag
                origin = jnp.where(flag > 0, origin, nothing)
                for turn in range(4):
                    built[source * CAP + k, rows[turn], :] = held[turn, origin]
        send(step).start()
        return place

    steps = WRITERS // SOURCES
    lax.fori_loop(0, steps, one, 0)
    for step in range(steps):
        send(step).wait()


def unpack(kept, parts, whole=None):
    sizes = [[piece.shape[0] for piece in part] for part in parts]
    operands = [piece for part in parts for piece in part] + ([] if whole is None else [whole])
    n_whole = 0 if whole is None else WHOLE
    width = operands[0].shape[-1]
    return pl.pallas_call(
        functools.partial(unpack_kernel, n_whole, sizes),
        in_specs=[HBM] * (1 + len(operands)),
        out_specs=HBM,
        out_shape=jax.ShapeDtypeStruct((SLOTS, width, width), jnp.bfloat16),
        scratch_shapes=[
            pltpu.VMEM((4, sum(sizes[0]) + 1 + WRITERS * n_whole, ROWS, width), jnp.bfloat16),
            pltpu.VMEM((SLOTS, width, width), jnp.bfloat16),
            pltpu.SemaphoreType.DMA((len(operands) + 4 * (WRITERS // SOURCES),)),
            pltpu.SemaphoreType.DMA((WRITERS // SOURCES,)),
            pltpu.SMEM(kept.shape, jnp.int32),
            pltpu.SemaphoreType.DMA,
        ],
        compiler_params=pltpu.CompilerParams(vmem_limit_bytes=VMEM),
        cost_estimate=cost(0, 0),
    )(kept, *operands)


def regroup(values):
    return lax.all_to_all(values, "fsdp", split_axis=0, concat_axis=0, tiled=True)


def upward(values):
    return lax.ppermute(values, "replica", [(i, (i + 1) % 4) for i in range(4)])


def downward(values):
    return lax.ppermute(values, "replica", [(i, (i - 1) % 4) for i in range(4)])


def along_z(first, second):
    first_up, first_down = upward(first), downward(first)
    second_up, second_down = upward(second), downward(second)
    return (first_up, second_down), ((first, second), (first_down, second_down), (upward(first_up), downward(second_down)), (first_up, second_up))


def along_z_in_turn(first, second):
    near = (upward(first), downward(second), downward(first), upward(second))
    first_up, second_down = after(near[0], near[2:]), after(near[1], near[2:])
    return ((first, second), (near[2], second_down), (upward(first_up), downward(second_down)), (first_up, near[3]))


def exchange_again(ticket, m_payload, w_payload, w_whole):
    *m_own, kept_w, kept_m, _, _ = pack_moment(FULL[0], ticket, m_payload)
    written_moment = unpack(kept_m, along_z(*m_own)[1])
    *w_own, _ = pack_weight(FULL[1], kept_w, w_payload)
    written_weight = unpack(kept_w, along_z(*w_own)[1], w_whole)
    return written_weight, written_moment


def on_device(weight, moment, base_codes, base_scale, weight_mask, moment_mask, writer):
    width = weight.shape[1]
    target = writer[:, 0]
    m_payload = regroup(moment_call(target, weight_mask, moment_mask, moment))
    w_payload, w_whole, refreshed = weight_call(target, weight_mask, base_scale, weight, base_codes)
    w_payload = regroup(after(w_payload, (m_payload,)))
    *m_own, kept_w, kept_m, totals, m_scales = pack_moment(USUAL[0], jnp.zeros((1,), jnp.int32), m_payload)
    m_near, m_parts = along_z(*m_own)
    w_whole = regroup(after(w_whole, (w_payload, *m_near)))
    *w_own, w_scales = pack_weight(USUAL[1], kept_w, w_payload)
    w_parts = along_z_in_turn(*w_own)
    written_moment = unpack(kept_m, m_parts)
    written_weight = unpack(kept_w, w_parts, w_whole)

    over = jnp.any(totals[:2, :WRITERS] >= jnp.array([[sum(USUAL[1])], [sum(USUAL[0])]], jnp.float32)).astype(jnp.int32)
    _, written_weight, written_moment = lax.while_loop(
        lambda carry: carry[0] < over,
        lambda carry: (carry[0] + 1, *exchange_again(carry[0].reshape(1), m_payload, w_payload, w_whole)),
        (jnp.int32(0), written_weight, written_moment),
    )
    written_scales = jnp.stack([w_scales[:, :CAP], m_scales[:, :CAP]], axis=0).astype(jnp.bfloat16)
    shape = (WRITERS, CAP, width, width)
    return written_weight.reshape(shape), written_moment.reshape(shape), written_scales, refreshed


def solution(mesh):
    placed = (
        P("fsdp", None, None),
        P("fsdp", None, None),
        P("fsdp", None, None),
        P("fsdp"),
        P("fsdp"),
        P("fsdp"),
        P("fsdp", None),
    )
    return jax.shard_map(
        on_device,
        mesh=mesh,
        in_specs=placed,
        out_specs=(
            P("fsdp", None, None, None),
            P("fsdp", None, None, None),
            P(None, "fsdp", None),
            P("fsdp", None, None),
        ),
        check_vma=False,
    )
```

```python
import functools

import jax
import jax.numpy as jnp
from jax import lax
from jax.experimental import pallas as pl
from jax.experimental.pallas import tpu as pltpu
from jax.sharding import PartitionSpec as P

EPSILON = 1e-06
WRITERS = 32
CAP = 8
GROUP = 8
GROUP_MOMENT = 16
ROWS = 32
TILE = 16
SLOTS = WRITERS * CAP
VMEM = 60 * 1024 * 1024
HBM = pl.BlockSpec(memory_space=pltpu.HBM)

WHOLE = 3
BY_ROWS_MOMENT = CAP
BY_ROWS_WEIGHT = CAP - WHOLE
USUAL = ((54, 54), (28, 28))
FULL = ((132, 132), (84, 84))


def clear(ref, length, value):
    def one(i, carry):
        ref[i] = value
        return carry

    lax.fori_loop(0, length, one, 0, unroll=8)


def scale_of(values):
    top = jnp.max(jnp.max(jnp.abs(values), axis=0, keepdims=True), axis=1, keepdims=True)
    top = jnp.broadcast_to(top + EPSILON, (8, 128))
    return top.astype(jnp.bfloat16).astype(jnp.float32)


def row_quarter():
    return pl.ds(pl.multiple_of(lax.axis_index("replica") * ROWS, ROWS), ROWS)


def payload_rows(by_rows):
    return by_rows * ROWS + TILE


def tile_rows(writer, by_rows):
    return pl.ds(pl.multiple_of(writer * payload_rows(by_rows) + by_rows * ROWS, TILE), TILE)


def slot_rows(writer, k, by_rows):
    return pl.ds(pl.multiple_of(writer * payload_rows(by_rows) + k * ROWS, TILE), ROWS)


def moment_kernel(
    writer_in, weight_mask_in, moment_mask_in, moment, payload, held, sems, tiles, totals, count, writer, weight_mask, moment_mask, scalar_sems
):
    rows = row_quarter()
    lane = lax.broadcasted_iota(jnp.int32, (8, 128), 1)
    line = lax.broadcasted_iota(jnp.int32, (8, 128), 0)
    steps = held.shape[0] // GROUP_MOMENT

    def fetch(step):
        part = pl.ds(step * GROUP_MOMENT, GROUP_MOMENT)
        return pltpu.make_async_copy(moment.at[part], held.at[part], sems.at[step])

    scalars = ((writer_in, writer), (weight_mask_in, weight_mask), (moment_mask_in, moment_mask))
    scalars = [pltpu.make_async_copy(source, there, scalar_sems.at[i]) for i, (source, there) in enumerate(scalars)]
    for copy in scalars:
        copy.start()
    for step in range(steps):
        fetch(step).start()
    clear(count, WRITERS, 0)
    tiles[...] = jnp.zeros(tiles.shape, tiles.dtype)
    totals[...] = jnp.zeros(totals.shape, totals.dtype)
    for copy in scalars:
        copy.wait()

    def one_step(step, carry):
        fetch(step).wait()
        total = totals[...]
        for i in range(GROUP_MOMENT):
            block = step * GROUP_MOMENT + i
            target = writer[block]
            rank = count[target]
            count[target] = rank + 1
            keep_w = weight_mask[block].astype(jnp.float32)
            keep_m = keep_w * moment_mask[block].astype(jnp.float32)
            total = total + jnp.where(lane == target, jnp.where(line == 3, keep_w, jnp.where(line == 4, keep_m, 0.0)), 0.0)
            scale = scale_of(held[block])
            kept = jnp.where(line == 0, scale, jnp.where(line == 1, keep_w, jnp.where(line == 2, keep_m, 0.0)))
            tiles[target] = jnp.where(lane == rank, kept, tiles[target])
            payload[slot_rows(target, rank, BY_ROWS_MOMENT), :] = (held[block, rows, :] * (keep_m / scale)[0:1, :]).astype(jnp.bfloat16)
        totals[...] = total
        return carry

    lax.fori_loop(0, steps, one_step, 0)
    common = totals[...]
    common = jnp.where(line == 3, jnp.maximum(common - WHOLE, 0.0), common)
    blank = jnp.zeros((TILE - 8, 128), jnp.float32)

    def one(w, carry):
        tile = jnp.concatenate([tiles[w] + common, blank], axis=0)
        payload[tile_rows(w, BY_ROWS_MOMENT), :] = tile.astype(jnp.bfloat16)
        return carry

    lax.fori_loop(0, WRITERS, one, 0, unroll=4)


def weight_kernel(blocks, writer, weight_mask, base_scale, weight, codes, payload, whole, refreshed, coded, scales, slot_of, kept_of, count, count_kept):
    step = pl.program_id(0)

    @pl.when(step == 0)
    def _():
        clear(slot_of, SLOTS, blocks)
        clear(kept_of, SLOTS, blocks)
        clear(count, WRITERS, 0)
        clear(count_kept, WRITERS, 0)
        coded[blocks] = jnp.zeros(coded.shape[1:], coded.dtype)
        scales[pl.ds(blocks, 8), :] = jnp.zeros((8, 128), jnp.float32)

    for i in range(GROUP):
        block = step * GROUP + i
        target = writer[block]
        rank = count[target]
        count[target] = rank + 1
        slot_of[target * CAP + rank] = block
        rank_kept = count_kept[target]
        count_kept[target] = rank_kept + weight_mask[block]
        kept_of[target * CAP + rank_kept] = block
        keep = weight_mask[block].astype(jnp.float32)
        base = codes[i].astype(jnp.float32) * base_scale[block]
        values = weight[i] - base
        scale = scale_of(values)
        scales[pl.ds(block, 1), :] = scale[0:1, :]
        rounded = (values * (keep / scale)[0:1, :]).astype(jnp.bfloat16)
        coded[block] = rounded
        refreshed[i] = (base + rounded.astype(jnp.float32) * scale[0:1, :]).astype(jnp.bfloat16)

    @pl.when(step == blocks // GROUP - 1)
    def _():
        rows = row_quarter()
        lane = lax.broadcasted_iota(jnp.int32, (TILE, 128), 1)

        def one(w, carry):
            tile = jnp.zeros((TILE, 128), jnp.float32)
            for k in range(CAP):
                block = kept_of[w * CAP + k]
                if k < WHOLE:
                    whole[w * WHOLE + k] = coded[block]
                else:
                    payload[slot_rows(w, k - WHOLE, BY_ROWS_WEIGHT), :] = coded[block, rows, :]
                scale = scales[pl.ds(slot_of[w * CAP + k], 1), :]
                tile = jnp.where(lane == k, jnp.broadcast_to(scale, (TILE, 128)), tile)
            payload[tile_rows(w, BY_ROWS_WEIGHT), :] = tile.astype(jnp.bfloat16)
            return carry

        lax.fori_loop(0, WRITERS, one, 0)


def cost(flops, moved):
    return pl.CostEstimate(flops=flops, bytes_accessed=moved, transcendentals=0)


def params():
    return pltpu.CompilerParams(dimension_semantics=("arbitrary",), vmem_limit_bytes=VMEM)


def moment_call(writer, weight_mask, moment_mask, moment):
    blocks, width = moment.shape[0], moment.shape[1]
    shape = (WRITERS * payload_rows(BY_ROWS_MOMENT), width)
    return pl.pallas_call(
        moment_kernel,
        in_specs=[HBM] * 4,
        out_shape=jax.ShapeDtypeStruct(shape, jnp.bfloat16),
        scratch_shapes=[
            pltpu.VMEM(moment.shape, jnp.float32),
            pltpu.SemaphoreType.DMA((blocks // GROUP_MOMENT,)),
            pltpu.VMEM((WRITERS, 8, 128), jnp.float32),
            pltpu.VMEM((8, 128), jnp.float32),
            pltpu.SMEM((WRITERS,), jnp.int32),
            pltpu.SMEM((blocks,), jnp.int32),
            pltpu.SMEM((blocks,), jnp.int32),
            pltpu.SMEM((blocks,), jnp.int32),
            pltpu.SemaphoreType.DMA((3,)),
        ],
        compiler_params=pltpu.CompilerParams(vmem_limit_bytes=VMEM),
        cost_estimate=cost(10 << 20, 12 << 20),
    )(writer, weight_mask, moment_mask, moment)


def weight_call(writer, weight_mask, base_scale, weight, codes):
    blocks, width = weight.shape[0], weight.shape[1]
    moving = pl.BlockSpec((GROUP, width, width), lambda i, *_: (i, 0, 0))
    payload = (WRITERS * payload_rows(BY_ROWS_WEIGHT), width)
    whole = (WRITERS * WHOLE, width, width)
    return pl.pallas_call(
        functools.partial(weight_kernel, blocks),
        grid_spec=pltpu.PrefetchScalarGridSpec(
            num_scalar_prefetch=3,
            grid=(blocks // GROUP,),
            in_specs=[moving, moving],
            out_specs=[pl.BlockSpec(payload, lambda i, *_: (0, 0)), pl.BlockSpec(whole, lambda i, *_: (0, 0, 0)), moving],
            scratch_shapes=[
                pltpu.VMEM((blocks + 1, width, width), jnp.bfloat16),
                pltpu.VMEM((blocks + 8, 128), jnp.float32),
                pltpu.SMEM((SLOTS,), jnp.int32),
                pltpu.SMEM((SLOTS,), jnp.int32),
                pltpu.SMEM((WRITERS,), jnp.int32),
                pltpu.SMEM((WRITERS,), jnp.int32),
            ],
        ),
        out_shape=[
            jax.ShapeDtypeStruct(payload, jnp.bfloat16),
            jax.ShapeDtypeStruct(whole, jnp.bfloat16),
            jax.ShapeDtypeStruct((blocks, width, width), jnp.bfloat16),
        ],
        compiler_params=params(),
        cost_estimate=cost(20 << 20, 28 << 20),
    )(writer, weight_mask, base_scale, weight, codes)


SOURCES = 8


def spread_lines(payload, by_rows, tiles, staged, spread, sems):
    copy = pltpu.make_async_copy(payload.at[:, pl.ds(by_rows * ROWS, TILE), :], tiles, sems.at[0])
    copy.start()
    copy.wait()
    line = lax.broadcasted_iota(jnp.int32, tiles.shape, 1)
    values = tiles[...].astype(jnp.float32)
    lines = [jnp.sum(jnp.where(line == i, values, 0.0), axis=1) for i in range(5)]
    for i in range(2):
        staged[i] = lines[1 + i].astype(jnp.int32)
    copy = pltpu.make_async_copy(staged, spread, sems.at[1])
    copy.start()
    copy.wait()
    return lines


def pack(by_rows, payload, held, packed, sems, advance):
    last = packed.shape[0] - 1
    steps = WRITERS // SOURCES

    def fetch(step):
        part = pl.ds(step * SOURCES, SOURCES)
        return pltpu.make_async_copy(payload.at[part], held.at[part], sems.at[step])

    for step in range(steps):
        fetch(step).start()
    yield

    def one(s, place):
        moves = advance(s)
        for k in range(by_rows):
            packed[jnp.minimum(place, last)] = held[s, pl.ds(k * ROWS, ROWS), :]
            place = place + moves[k]
        return place

    place = 0
    for step in range(steps):
        fetch(step).wait()
        place = lax.fori_loop(step * SOURCES, (step + 1) * SOURCES, one, place)
    yield


def share(packed, own):
    start = 0
    for part in own:
        part[...] = packed[start : start + part.shape[0]]
        start += part.shape[0]


def pack_moment_kernel(ticket, payload, *refs):
    *own, kept_w, kept_m, totals, scales, held, packed, tiles, staged, spread, sems, tile_sems = refs
    steps = pack(BY_ROWS_MOMENT, payload, held, packed, sems, lambda s: [spread[1, s, k] for k in range(CAP)])
    next(steps)
    lines = spread_lines(payload, BY_ROWS_MOMENT, tiles, staged, spread, tile_sems)
    next(steps)
    share(packed, own)
    scales[...] = lines[0]
    kept_w[...] = lines[1].astype(jnp.int32)
    kept_m[...] = lines[2].astype(jnp.int32)
    row = lax.broadcasted_iota(jnp.int32, (8, 128), 0)
    total_w, total_m = (jnp.sum(lines[i], axis=0, keepdims=True) for i in (3, 4))
    totals[...] = jnp.where(row == 0, total_w, jnp.where(row == 1, total_m, 0.0))


def pack_moment(capacity, ticket, payload):
    width = payload.shape[-1]
    parts = [jax.ShapeDtypeStruct((size, ROWS, width), jnp.bfloat16) for size in capacity]
    flags = jax.ShapeDtypeStruct((WRITERS, width), jnp.int32)
    return pl.pallas_call(
        pack_moment_kernel,
        in_specs=[HBM, HBM],
        out_shape=[
            *parts,
            flags,
            flags,
            jax.ShapeDtypeStruct((8, width), jnp.float32),
            jax.ShapeDtypeStruct((WRITERS, width), jnp.float32),
        ],
        scratch_shapes=[
            pltpu.VMEM((WRITERS, payload_rows(BY_ROWS_MOMENT), width), jnp.bfloat16),
            pltpu.VMEM((sum(capacity), ROWS, width), jnp.bfloat16),
            pltpu.VMEM((WRITERS, TILE, width), jnp.bfloat16),
            pltpu.VMEM((2, WRITERS, width), jnp.int32),
            pltpu.SMEM((2, WRITERS, width), jnp.int32),
            pltpu.SemaphoreType.DMA((WRITERS // SOURCES,)),
            pltpu.SemaphoreType.DMA((2,)),
        ],
        compiler_params=pltpu.CompilerParams(vmem_limit_bytes=VMEM),
        cost_estimate=cost(0, 0),
    )(ticket, payload.reshape(WRITERS, -1, width))


def pack_weight_kernel(kept_in, payload, *refs):
    *own, scales, held, packed, sems, kept, kept_sem = refs
    copy = pltpu.make_async_copy(kept_in, kept, kept_sem)
    copy.start()

    def advance(s):
        found = functools.reduce(jnp.add, [kept[s, k] for k in range(CAP)])
        return [jnp.where(found > WHOLE + k, 1, 0) for k in range(BY_ROWS_WEIGHT)]

    steps = pack(BY_ROWS_WEIGHT, payload, held, packed, sems, advance)
    next(steps)
    copy.wait()
    next(steps)
    share(packed, own)
    scales[...] = held[:, pl.ds(BY_ROWS_WEIGHT * ROWS, TILE), :].astype(jnp.float32)[:, 0, :]


def pack_weight(capacity, kept, payload):
    width = payload.shape[-1]
    parts = [jax.ShapeDtypeStruct((size, ROWS, width), jnp.bfloat16) for size in capacity]
    return pl.pallas_call(
        pack_weight_kernel,
        in_specs=[HBM, HBM],
        out_shape=[*parts, jax.ShapeDtypeStruct((WRITERS, width), jnp.float32)],
        scratch_shapes=[
            pltpu.VMEM((WRITERS, payload_rows(BY_ROWS_WEIGHT), width), jnp.bfloat16),
            pltpu.VMEM((sum(capacity), ROWS, width), jnp.bfloat16),
            pltpu.SemaphoreType.DMA((WRITERS // SOURCES,)),
            pltpu.SMEM(kept.shape, jnp.int32),
            pltpu.SemaphoreType.DMA,
        ],
        compiler_params=pltpu.CompilerParams(vmem_limit_bytes=VMEM),
        cost_estimate=cost(0, 0),
    )(kept, payload.reshape(WRITERS, -1, width))


def after_kernel(*refs):
    pass


def after(values, earlier):
    return pl.pallas_call(
        after_kernel,
        in_specs=[HBM] * (1 + len(earlier)),
        out_specs=HBM,
        out_shape=jax.ShapeDtypeStruct(values.shape, values.dtype),
        input_output_aliases={0: 0},
        compiler_params=pltpu.CompilerParams(vmem_limit_bytes=VMEM),
    )(values, *earlier)


def unpack_kernel(n_whole, sizes, kept_in, *refs):
    out, held, built, sems, out_sems, kept, kept_sem = refs[-7:]
    replica = lax.axis_index("replica")
    copy_kept = pltpu.make_async_copy(kept_in, kept, kept_sem)
    copy_kept.start()
    nothing = sum(sizes[0])
    first_whole = nothing + 1
    rows = [pl.ds(pl.multiple_of(lax.rem(replica + turn, 4) * ROWS, ROWS), ROWS) for turn in range(4)]
    copies = []
    for turn in range(4):
        start = 0
        for size in sizes[turn]:
            i = len(copies)
            copies.append(pltpu.make_async_copy(refs[i], held.at[turn, pl.ds(start, size)], sems.at[i]))
            start += size
    whole = refs[len(copies)] if n_whole else None

    def fetch_whole(step, turn):
        size = SOURCES * n_whole
        there = held.at[turn, pl.ds(first_whole + step * size, size)]
        return pltpu.make_async_copy(whole.at[pl.ds(step * size, size), rows[turn], :], there, sems.at[len(copies) + 4 * step + turn])

    for copy in copies:
        copy.start()
    if n_whole:
        for step in range(WRITERS // SOURCES):
            for turn in range(4):
                fetch_whole(step, turn).start()
    for turn in range(4):
        held[turn, nothing] = jnp.zeros(held.shape[2:], held.dtype)
    copy_kept.wait()
    for copy in copies:
        copy.wait()

    def send(step):
        part = pl.ds(step * SOURCES * CAP, SOURCES * CAP)
        return pltpu.make_async_copy(built.at[part], out.at[part], out_sems.at[step])

    def one(step, place):
        if n_whole:
            for turn in range(4):
                fetch_whole(step, turn).wait()
        for s in range(SOURCES):
            source = step * SOURCES + s
            rank = 0
            for k in range(CAP):
                flag = kept[source, k]
                origin = jnp.minimum(place, nothing - 1)
                if n_whole:
                    as_whole = rank < n_whole
                    origin = jnp.where(as_whole, first_whole + source * n_whole + rank, origin)
                    place = place + jnp.where(as_whole, 0, flag)
                    rank = rank + flag
                else:
                    place = place + flag
                origin = jnp.where(flag > 0, origin, nothing)
                for turn in range(4):
                    built[source * CAP + k, rows[turn], :] = held[turn, origin]
        send(step).start()
        return place

    steps = WRITERS // SOURCES
    lax.fori_loop(0, steps, one, 0)
    for step in range(steps):
        send(step).wait()


def unpack(kept, parts, whole=None):
    sizes = [[piece.shape[0] for piece in part] for part in parts]
    operands = [piece for part in parts for piece in part] + ([] if whole is None else [whole])
    n_whole = 0 if whole is None else WHOLE
    width = operands[0].shape[-1]
    return pl.pallas_call(
        functools.partial(unpack_kernel, n_whole, sizes),
        in_specs=[HBM] * (1 + len(operands)),
        out_specs=HBM,
        out_shape=jax.ShapeDtypeStruct((SLOTS, width, width), jnp.bfloat16),
        scratch_shapes=[
            pltpu.VMEM((4, sum(sizes[0]) + 1 + WRITERS * n_whole, ROWS, width), jnp.bfloat16),
            pltpu.VMEM((SLOTS, width, width), jnp.bfloat16),
            pltpu.SemaphoreType.DMA((len(operands) + 4 * (WRITERS // SOURCES),)),
            pltpu.SemaphoreType.DMA((WRITERS // SOURCES,)),
            pltpu.SMEM(kept.shape, jnp.int32),
            pltpu.SemaphoreType.DMA,
        ],
        compiler_params=pltpu.CompilerParams(vmem_limit_bytes=VMEM),
        cost_estimate=cost(0, 0),
    )(kept, *operands)


def regroup(values):
    return lax.all_to_all(values, "fsdp", split_axis=0, concat_axis=0, tiled=True)


def upward(values):
    return lax.ppermute(values, "replica", [(i, (i + 1) % 4) for i in range(4)])


def downward(values):
    return lax.ppermute(values, "replica", [(i, (i - 1) % 4) for i in range(4)])


def along_z(first, second):
    first_up, first_down = upward(first), downward(first)
    second_up, second_down = upward(second), downward(second)
    return (first_up, second_down), ((first, second), (first_down, second_down), (upward(first_up), downward(second_down)), (first_up, second_up))


def exchange_again(ticket, m_payload, w_payload, w_whole):
    *m_own, kept_w, kept_m, _, _ = pack_moment(FULL[0], ticket, m_payload)
    written_moment = unpack(kept_m, along_z(*m_own)[1])
    *w_own, _ = pack_weight(FULL[1], kept_w, w_payload)
    written_weight = unpack(kept_w, along_z(*w_own)[1], w_whole)
    return written_weight, written_moment


def on_device(weight, moment, base_codes, base_scale, weight_mask, moment_mask, writer):
    width = weight.shape[1]
    target = writer[:, 0]
    m_payload = regroup(moment_call(target, weight_mask, moment_mask, moment))
    w_payload, w_whole, refreshed = weight_call(target, weight_mask, base_scale, weight, base_codes)
    w_payload = regroup(after(w_payload, (m_payload,)))
    *m_own, kept_w, kept_m, totals, m_scales = pack_moment(USUAL[0], jnp.zeros((1,), jnp.int32), m_payload)
    m_near, m_parts = along_z(*m_own)
    w_whole = regroup(after(w_whole, (w_payload, *m_near)))
    *w_own, w_scales = pack_weight(USUAL[1], kept_w, w_payload)
    w_parts = along_z(*w_own)[1]
    written_moment = unpack(kept_m, m_parts)
    written_weight = unpack(kept_w, w_parts, w_whole)

    over = jnp.any(totals[:2, :WRITERS] >= jnp.array([[sum(USUAL[1])], [sum(USUAL[0])]], jnp.float32)).astype(jnp.int32)
    _, written_weight, written_moment = lax.while_loop(
        lambda carry: carry[0] < over,
        lambda carry: (carry[0] + 1, *exchange_again(carry[0].reshape(1), m_payload, w_payload, w_whole)),
        (jnp.int32(0), written_weight, written_moment),
    )
    written_scales = jnp.stack([w_scales[:, :CAP], m_scales[:, :CAP]], axis=0).astype(jnp.bfloat16)
    shape = (WRITERS, CAP, width, width)
    return written_weight.reshape(shape), written_moment.reshape(shape), written_scales, refreshed


def solution(mesh):
    placed = (
        P("fsdp", None, None),
        P("fsdp", None, None),
        P("fsdp", None, None),
        P("fsdp"),
        P("fsdp"),
        P("fsdp"),
        P("fsdp", None),
    )
    return jax.shard_map(
        on_device,
        mesh=mesh,
        in_specs=placed,
        out_specs=(
            P("fsdp", None, None, None),
            P("fsdp", None, None, None),
            P(None, "fsdp", None),
            P("fsdp", None, None),
        ),
        check_vma=False,
    )
```
